512 devices in a mesh: dp: 16 (over y, core), fsdp: 32 (over x, z).
Axes of the slice: x: 4, y: 8, z: 8, core: 2. Of those that a mesh axis runs over, the one named last changes fastest.
Arguments:
- tokens: bfloat16 [49152, 8192], P('dp', 'fsdp'), may hold values from -6 to 6
- cotangent: bfloat16 [49152, 8192], P('dp', 'fsdp'), may hold values from -0.02734375 to 0.02734375
- projection: bfloat16 [8192, 512], P('fsdp'), may hold values from -0.0625 to 0.0625
- weight: bfloat16 [8192, 8192], P('dp', 'fsdp'), may hold values from -0.0625 to 0.0625
- first_moment: float32 [512, 8192], P('dp', 'fsdp'), may hold values from -6 to 6
- second_moment: float32 [512, 8192], P('dp', 'fsdp'), may hold values from 0.25 to 4
Outputs:
- new_weight: bfloat16 [8192, 8192], P('dp', 'fsdp')
- new_first: float32 [512, 8192], P('dp', 'fsdp')
- new_second: float32 [512, 8192], P('dp', 'fsdp')
The draws below stay inside these ranges and needn't reach their ends.
All inputs are finite; a program needn't handle non-finite values.
Results may differ from the reference program's by a relative error of at most 0.0065.
Values may be sent and summed in bfloat16 or wider, within the bound.
A program may use at most 64 MiB of HBM per device.

```python
import math
import jax
import jax.numpy as jnp
from jax import lax

D = 8192
R = 512
STEP = 10
TOKENS = 49152
N_FSDP = 32


def block_levels(stream_key, shape, cuts, smallest, largest):
    def one(dim, parts):
        draws = jax.random.uniform(jax.random.fold_in(jax.random.fold_in(stream_key, 6), dim), (parts,), jnp.float32, smallest / len(cuts), largest / len(cuts))
        return jnp.repeat(jnp.exp(draws), shape[dim] // parts).reshape((-1,) + (1,) * (len(shape) - dim - 1))

    level = one(*cuts[0])
    for cut in cuts[1:]:
        level = level * one(*cut)
    return level


def bell_draw(rng, extent, spread, limit, split=(), dtype=jnp.bfloat16):
    values = jax.random.normal(rng, extent, jnp.float32) * spread
    if len(split) > 0:
        values = block_levels(rng, extent, split, -0.22, 0.18) * values
    return jnp.clip(values, min=-limit, max=limit).astype(dtype)


def setup_inputs(seed: int = 0) -> dict:
    arg_keys = jax.random.split(jax.random.key(seed), 7)
    tokens = bell_draw(arg_keys[0], (TOKENS, D), 1.0, 6.0, ((0, 16), (1, 32)))
    cotangent = bell_draw(arg_keys[1], (TOKENS, D), TOKENS ** -0.5, 0.02734375, ((0, 16), (1, 32)))
    projection = bell_draw(arg_keys[2], (D, R), D ** -0.5, 0.0625, ((0, 32),))
    weight = bell_draw(arg_keys[3], (D, D), D ** -0.5, 0.0625, ((0, 16), (1, 32)))
    first_moment = bell_draw(arg_keys[4], (R, D), 1.0, 6.0, ((0, 16), (1, 32)), jnp.float32)
    second_moment = jnp.clip(jnp.exp(math.log(4.0) - 2.7725887 * jax.random.uniform(arg_keys[5], (R, D), jnp.float32) ** block_levels(arg_keys[5], (R, D), ((0, 16), (1, 32)), -0.2, 0.2)), 0.25, 4.0)
    return dict(tokens=tokens, cotangent=cotangent, projection=projection, weight=weight, first_moment=first_moment, second_moment=second_moment)


BETA_ONE = 0.9
BETA_TWO = 0.999
EPSILON = 1e-08
RATE = 0.1

def reference(tokens, cotangent, projection, weight, first_moment, second_moment):
    width = D // N_FSDP

    def add_block(index, total):
        start = (index * width).astype(jnp.int32)
        columns = lax.dynamic_slice_in_dim(tokens, start, width, 1)
        rows = lax.dynamic_slice_in_dim(projection, start, width, 0)
        rounded = lax.optimization_barrier(jnp.dot(columns, rows, preferred_element_type=jnp.float32).astype(jnp.bfloat16))
        return total + rounded.astype(jnp.float32)
    summed = lax.fori_loop(0, N_FSDP, add_block, jnp.zeros((TOKENS, R), jnp.float32))
    reduced = summed.astype(jnp.bfloat16)
    gradient = jnp.dot(reduced.T, cotangent, preferred_element_type=jnp.float32)
    new_first = BETA_ONE * first_moment + (1.0 - BETA_ONE) * gradient
    new_second = BETA_TWO * second_moment + (1.0 - BETA_TWO) * gradient * gradient
    first_fix = 1.0 - BETA_ONE ** STEP
    second_fix = 1.0 - BETA_TWO ** STEP
    direction = (new_first / first_fix / (jnp.sqrt(new_second / second_fix) + EPSILON)).astype(jnp.bfloat16)
    update = jnp.dot(projection, direction, preferred_element_type=jnp.float32)
    new_weight = (weight.astype(jnp.float32) - RATE * update).astype(jnp.bfloat16)
    return (new_weight, new_first, new_second)
```

```python
import functools

import jax
import jax.numpy as jnp
from jax import lax
from jax.experimental import pallas as pl
from jax.experimental.pallas import tpu as pltpu
from jax.sharding import PartitionSpec as P

STEP = 10
BETA_ONE = 0.9
BETA_TWO = 0.999
EPSILON = 1e-08
RATE = 0.1

NX, NY, NZ = 4, 8, 8
RANK = 512
WIDTH = 256
QUARTER = 768
CHUNKS = 3
TC = QUARTER // CHUNKS
MESH = pl.DeviceIdType.MESH
F32 = jnp.float32
BF16 = jnp.bfloat16


def kernel(
    tok, cot, proj, wgt, m1, m2, nw, n1, n2,
    pt, t4, c4, psend, zr, ag, acc, gs, gc, xs, xr, ysum, ys, yr, dirb, pu1, pu2, pu3,
    lsem, pts, ptr, pcs, pcr, ts, tr, cs, cr, zs_, zr_, as_, ar_, gcs, gcr, xss, xsr, yss, ysr,
    ds_, dr_, dcs, dcr, u1s, u1r, u2s, u2r, u3s, u3r,
):
    dp = lax.axis_index("dp")
    fs = lax.axis_index("fsdp")
    y, c = dp // 2, lax.rem(dp, 2)
    x, z = fs // NZ, lax.rem(fs, NZ)
    o = 1 - c

    def px(d):
        return (dp, lax.rem(x + d + NX, NX) * NZ + z)

    def pz(d):
        return (dp, x * NZ + lax.rem(z + d + NZ, NZ))

    def py(d, other=False):
        return (lax.rem(y + d + NY, NY) * 2 + (o if other else c), fs)

    sent = []

    def put(src, dst, ssem, rsem, dev):
        cp = pltpu.make_async_remote_copy(
            src_ref=src, dst_ref=dst, send_sem=ssem, recv_sem=rsem, device_id=dev, device_id_type=MESH
        )
        cp.start()
        sent.append(cp)

    def got(dst, ssem, rsem):
        pltpu.make_async_remote_copy(
            src_ref=dst, dst_ref=dst, send_sem=ssem, recv_sem=rsem, device_id=(dp, fs), device_id_type=MESH
        ).wait_recv()

    own_t = pltpu.make_async_copy(tok.at[pl.ds(x * QUARTER, QUARTER)], t4.at[0], lsem.at[0])
    own_c = pltpu.make_async_copy(cot.at[pl.ds(x * QUARTER, QUARTER)], c4.at[0], lsem.at[1])
    own_t.start()
    own_c.start()

    barrier = pltpu.get_barrier_semaphore()
    for d in range(1, NX):
        pl.semaphore_signal(barrier, inc=1, device_id=px(d), device_id_type=MESH)
    for d in range(1, NZ):
        pl.semaphore_signal(barrier, inc=1, device_id=pz(d), device_id_type=MESH)
    for d in range(NY):
        pl.semaphore_signal(barrier, inc=1, device_id=py(d, True), device_id_type=MESH)
        if d:
            pl.semaphore_signal(barrier, inc=1, device_id=py(d), device_id_type=MESH)
    pt[0] = proj[...].T
    pu1[x] = proj[pl.ds(dp * 16, 16)]
    pl.semaphore_wait(barrier, NX - 1 + NZ - 1 + 2 * NY - 1)

    mine, theirs = pl.ds(c * 256, 256), pl.ds(o * 256, 256)
    for d in (2, 1, 3):
        put(pt.at[0, mine], pt.at[d, mine], pts.at[d], ptr.at[d], px(d))
    for d in (2, 1, 3):
        put(pu1.at[x], pu1.at[x], u1s.at[d], u1r.at[d], px(d))
    for k in range(CHUNKS):
        for d in (2, 1, 3):
            rows = pl.ds(lax.rem(x + d, NX) * QUARTER + k * TC, TC)
            put(tok.at[rows], t4.at[d, pl.ds(k * TC, TC)], ts.at[k, d], tr.at[k, d], px(d))

    for d in (1, 3, 2):
        got(pt.at[d, mine], pts.at[d], ptr.at[d])
        put(pt.at[d, mine], pt.at[d, mine], pcs.at[d], pcr.at[d], py(0, True))
    for d in (1, 3, 2):
        got(pu1.at[lax.rem(x - d + NX, NX)], u1s.at[d], u1r.at[d])
    for d in range(1, NZ):
        put(pu1, pu2.at[z], u2s.at[d], u2r.at[d], pz(d))
    pu2[z] = pu1[...]
    for d in (1, 3, 2):
        got(pt.at[d, theirs], pcs.at[d], pcr.at[d])
    own_t.wait()

    def send_cot():
        for k in range(CHUNKS):
            for d in (2, 1, 3):
                rows = pl.ds(lax.rem(x + d, NX) * QUARTER + k * TC, TC)
                put(cot.at[rows], c4.at[d, pl.ds(k * TC, TC)], cs.at[k, d], cr.at[k, d], px(d))

    def partial(k):
        rows = pl.ds(k * TC, TC)
        for d in (1, 3, 2):
            got(t4.at[d, rows], ts.at[k, d], tr.at[k, d])
        low = None
        for d in range(NX):
            part = lax.dot_general(
                pt[d], t4[d, rows], (((1,), (1,)), ((), ())), preferred_element_type=F32
            )
            low = part if low is None else low + part
        psend[k] = low.astype(BF16).reshape(NZ, RANK // NZ, TC)
        for d in (4, 3, 5, 2, 6, 1, 7):
            put(psend.at[k, lax.rem(z + d, NZ)], zr.at[k, d], zs_.at[k, d], zr_.at[k, d], pz(d))

    def reduce(k):
        total = psend[k, z].astype(F32)
        for d in (1, 7, 2, 6, 3, 5, 4):
            got(zr.at[k, d], zs_.at[k, d], zr_.at[k, d])
            total = total + zr[k, d].astype(F32)
        ag[k, z] = total.astype(BF16)
        for d in (4, 3, 5, 2, 6, 1, 7):
            put(ag.at[k, z], ag.at[k, z], as_.at[k, d], ar_.at[k, d], pz(d))

    def send_update_rows():
        for d in range(1, NZ):
            got(pu2.at[lax.rem(z - d + NZ, NZ)], u2s.at[d], u2r.at[d])
        for d in range(NY):
            for e in range(2):
                peer = lax.rem(y + d, NY) * 2 + (o if e else c)
                src = pu2.at[pl.ds(2 * lax.rem(peer, 4), 2), peer // 4]
                if d == 0 and e == 0:
                    pu3[:, dp] = pu2[pl.ds(2 * lax.rem(peer, 4), 2), peer // 4]
                else:
                    put(src, pu3.at[:, dp], u3s.at[d, e], u3r.at[d, e], py(d, e == 1))

    for k in range(CHUNKS):
        partial(k)
        if k == CHUNKS - 2:
            send_cot()
        if k >= 1:
            reduce(k - 1)
        if k == 0:
            send_update_rows()
    reduce(CHUNKS - 1)

    own_c.wait()
    for k in range(CHUNKS):
        rows = pl.ds(k * TC, TC)
        for d in (1, 7, 2, 6, 3, 5, 4):
            got(ag.at[k, lax.rem(z - d + NZ, NZ)], as_.at[k, d], ar_.at[k, d])
        low = ag[k].reshape(RANK, TC)
        for d in (0, 1, 3, 2):
            if d:
                got(c4.at[d, rows], cs.at[k, d], cr.at[k, d])
            part = jnp.dot(low, c4[d, rows], preferred_element_type=F32).reshape(NY, 2, 32, WIDTH)
            acc[d] = part if k == 0 else acc[d] + part

    for d in (2, 1, 3, 0):
        gs[d] = acc[d, :, o].astype(BF16)
        put(gs.at[d], gc.at[d], gcs.at[d], gcr.at[d], py(0, True))
    for d in (2, 1, 3):
        got(gc.at[d], gcs.at[d], gcr.at[d])
        xs[d] = (acc[d, :, c] + gc[d].astype(F32)).astype(BF16)
        put(xs.at[d], xr.at[d], xss.at[d], xsr.at[d], px(-d))
    got(gc.at[0], gcs.at[0], gcr.at[0])
    total = acc[0, :, c] + gc[0].astype(F32)
    for d in (1, 3, 2):
        got(xr.at[d], xss.at[d], xsr.at[d])
        total = total + xr[d].astype(F32)
    ysum[...] = total
    ys[...] = total.astype(BF16)
    for d in (4, 3, 5, 2, 6, 1, 7):
        put(ys.at[lax.rem(y + d, NY)], yr.at[d], yss.at[d], ysr.at[d], py(d))
    gradient = ysum[y]
    for d in (1, 7, 2, 6, 3, 5, 4):
        got(yr.at[d], yss.at[d], ysr.at[d])
        gradient = gradient + yr[d].astype(F32)

    new_first = BETA_ONE * m1[...] + (1.0 - BETA_ONE) * gradient
    new_second = BETA_TWO * m2[...] + (1.0 - BETA_TWO) * gradient * gradient
    first_fix = 1.0 - BETA_ONE**STEP
    second_fix = 1.0 - BETA_TWO**STEP
    direction = new_first / first_fix / (jnp.sqrt(new_second / second_fix) + EPSILON)
    dirb[dp] = direction.astype(BF16)
    for d in (4, 3, 5, 2, 6, 1, 7):
        put(dirb.at[dp], dirb.at[dp], ds_.at[d], dr_.at[d], py(d))
    put(dirb.at[dp], dirb.at[dp], dcs.at[0], dcr.at[0], py(0, True))
    n1[...] = new_first
    n2[...] = new_second
    for d in range(NY):
        for e in range(2):
            if d or e:
                peer = lax.rem(y - d + NY, NY) * 2 + (o if e else c)
                got(pu3.at[:, peer], u3s.at[d, e], u3r.at[d, e])
    for d in (1, 7, 2, 6, 3, 5, 4):
        slot = lax.rem(y - d + NY, NY) * 2 + c
        got(dirb.at[slot], ds_.at[d], dr_.at[d])
        put(dirb.at[slot], dirb.at[slot], dcs.at[d], dcr.at[d], py(0, True))
    for d in (0, 1, 7, 2, 6, 3, 5, 4):
        slot = lax.rem(y - d + NY, NY) * 2 + o
        got(dirb.at[slot], dcs.at[d], dcr.at[d])
    update = jnp.dot(
        pu3[...].reshape(RANK, RANK), dirb[...].reshape(RANK, WIDTH), preferred_element_type=F32
    )
    nw[...] = (wgt[...].astype(F32) - RATE * update).astype(BF16)
    for cp in sent:
        cp.wait_send()


def shards(tokens, cotangent, projection, weight, first_moment, second_moment):
    vmem = pl.BlockSpec(memory_space=pltpu.VMEM)
    hbm = pl.BlockSpec(memory_space=pl.ANY)
    dma = pltpu.SemaphoreType.DMA
    v = pltpu.VMEM
    scratch = [
        v((NX, RANK, WIDTH), BF16),
        v((NX, QUARTER, WIDTH), BF16),
        v((NX, QUARTER, WIDTH), BF16),
        v((CHUNKS, NZ, RANK // NZ, TC), BF16),
        v((CHUNKS, NZ, RANK // NZ, TC), BF16),
        v((CHUNKS, NZ, RANK // NZ, TC), BF16),
        v((NX, NY, 2, 32, WIDTH), F32),
        v((NX, NY, 32, WIDTH), BF16),
        v((NX, NY, 32, WIDTH), BF16),
        v((NX, NY, 32, WIDTH), BF16),
        v((NX, NY, 32, WIDTH), BF16),
        v((NY, 32, WIDTH), F32),
        v((NY, 32, WIDTH), BF16),
        v((NY, 32, WIDTH), BF16),
        v((2 * NY, 32, WIDTH), BF16),
        v((NX, 16, RANK), BF16),
        v((NZ, NX, 16, RANK), BF16),
        v((2, 16, 16, RANK), BF16),
        dma((2,)),
        dma((NX,)), dma((NX,)), dma((NX,)), dma((NX,)),
        dma((CHUNKS, NX)), dma((CHUNKS, NX)), dma((CHUNKS, NX)), dma((CHUNKS, NX)),
        dma((CHUNKS, NZ)), dma((CHUNKS, NZ)), dma((CHUNKS, NZ)), dma((CHUNKS, NZ)),
        dma((NX,)), dma((NX,)), dma((NX,)), dma((NX,)),
        dma((NY,)), dma((NY,)), dma((NY,)), dma((NY,)), dma((NY,)), dma((NY,)),
        dma((NX,)), dma((NX,)), dma((NZ,)), dma((NZ,)), dma((NY, 2)), dma((NY, 2)),
    ]
    return pl.pallas_call(
        kernel,
        out_shape=(
            jax.ShapeDtypeStruct(weight.shape, weight.dtype),
            jax.ShapeDtypeStruct(first_moment.shape, F32),
            jax.ShapeDtypeStruct(second_moment.shape, F32),
        ),
        in_specs=[hbm, hbm, vmem, vmem, vmem, vmem],
        out_specs=(vmem, vmem, vmem),
        scratch_shapes=scratch,
        compiler_params=pltpu.CompilerParams(
            collective_id=0, has_side_effects=True, vmem_limit_bytes=48 * 2**20
        ),
        cost_estimate=pl.CostEstimate(flops=1_800_000_000, bytes_accessed=4_500_000, transcendentals=8192),
    )(tokens, cotangent, projection, weight, first_moment, second_moment)


def solution(mesh):
    return jax.shard_map(
        shards,
        mesh=mesh,
        in_specs=(
            P("dp", "fsdp"),
            P("dp", "fsdp"),
            P("fsdp", None),
            P("dp", "fsdp"),
            P("dp", "fsdp"),
            P("dp", "fsdp"),
        ),
        out_specs=(P("dp", "fsdp"), P("dp", "fsdp"), P("dp", "fsdp")),
        check_vma=False,
    )
```

```python
import functools

import jax
import jax.numpy as jnp
from jax import lax
from jax.experimental import pallas as pl
from jax.experimental.pallas import tpu as pltpu
from jax.sharding import PartitionSpec as P

STEP = 10
BETA_ONE = 0.9
BETA_TWO = 0.999
EPSILON = 1e-08
RATE = 0.1

NX, NY, NZ = 4, 8, 8
RANK = 512
WIDTH = 256
QUARTER = 768
SIZES = (256, 256, 256)
CHUNKS = len(SIZES)
STARTS = tuple(sum(SIZES[:k]) for k in range(CHUNKS))
MESH = pl.DeviceIdType.MESH
F32 = jnp.float32
BF16 = jnp.bfloat16


def kernel(
    tok, cot, proj_hbm, wgt_hbm, m1_hbm, m2_hbm, nw, n1, n2,
    proj, wgt, m1, m2, pt, t4, c4, psend, zr, zq, ag, acc, gs, gc, xs, xr, ysum, ys, yr, dirb,
    pu1, pu2, pu3, lsem, s_pt, s_py, s_pc, s_t, s_c, s_z, s_a, s_g, s_x, s_y, s_d, s_dc, s_u1, s_u2, s_u3,
):
    dp = lax.axis_index("dp")
    fs = lax.axis_index("fsdp")
    y, c = dp // 2, lax.rem(dp, 2)
    x, z = fs // NZ, lax.rem(fs, NZ)
    o = 1 - c

    def px(d):
        return (dp, lax.rem(x + d + NX, NX) * NZ + z)

    def pz(d):
        return (dp, x * NZ + lax.rem(z + d + NZ, NZ))

    def py(d, other=False):
        return (lax.rem(y + d + NY, NY) * 2 + (o if other else c), fs)

    sent = []

    def put(src, dst, sems, at, dev):
        cp = pltpu.make_async_remote_copy(
            src_ref=src, dst_ref=dst, send_sem=sems[0].at[at], recv_sem=sems[1].at[at], device_id=dev, device_id_type=MESH
        )
        cp.start()
        sent.append(cp)

    def got(dst, sems, at):
        pltpu.make_async_remote_copy(
            src_ref=dst, dst_ref=dst, send_sem=sems[0].at[at], recv_sem=sems[1].at[at], device_id=(dp, fs), device_id_type=MESH
        ).wait_recv()

    own_t = pltpu.make_async_copy(tok.at[pl.ds(x * QUARTER, QUARTER)], t4.at[0], lsem.at[0])
    own_c = pltpu.make_async_copy(cot.at[pl.ds(x * QUARTER, QUARTER)], c4.at[0], lsem.at[1])
    loads = [
        pltpu.make_async_copy(src, dst, lsem.at[i + 2])
        for i, (src, dst) in enumerate(((proj_hbm, proj), (wgt_hbm, wgt), (m1_hbm, m1), (m2_hbm, m2)))
    ]
    for load in loads:
        load.start()
    own_t.start()
    own_c.start()

    barrier = pltpu.get_barrier_semaphore()
    for d in range(1, NX):
        pl.semaphore_signal(barrier, inc=1, device_id=px(d), device_id_type=MESH)
    for d in range(1, NZ):
        pl.semaphore_signal(barrier, inc=1, device_id=pz(d), device_id_type=MESH)
    for d in range(NY):
        pl.semaphore_signal(barrier, inc=1, device_id=py(d, True), device_id_type=MESH)
        if d:
            pl.semaphore_signal(barrier, inc=1, device_id=py(d), device_id_type=MESH)
    loads[0].wait()
    pt[0] = proj[...].T
    pu1[x] = proj[pl.ds(dp * 16, 16)]
    pl.semaphore_wait(barrier, NX - 1 + NZ - 1 + 2 * NY - 1)

    def ranks(core, row):
        return pl.ds(core * 256 + lax.rem(row + NY, 4) * 64, 64)

    others = pl.ds(1, NX - 1)
    for d in (2, 1, 3):
        put(pt.at[0, ranks(c, y)], pt.at[d, ranks(c, y)], s_pt, (d,), px(d))
    for d in (2, 1, 3):
        put(pu1.at[x], pu1.at[x], s_u1, (d,), px(d))
    for k in range(CHUNKS):
        for d in (2, 1, 3):
            rows = pl.ds(lax.rem(x + d, NX) * QUARTER + STARTS[k], SIZES[k])
            put(tok.at[rows], t4.at[d, pl.ds(STARTS[k], SIZES[k])], s_t, (k, d), px(d))

    for d in (1, 3, 2):
        got(pt.at[d, ranks(c, y)], s_pt, (d,))
    far = 2 - 4 * c
    for i, d in enumerate((1, -1, far)):
        put(pt.at[others, ranks(c, y)], pt.at[others, ranks(c, y)], s_py, (i,), py(d))
    put(pt.at[others, ranks(c, y)], pt.at[others, ranks(c, y)], s_pc, (3,), py(0, True))

    for d in (1, 3, 2):
        got(pu1.at[lax.rem(x - d + NX, NX)], s_u1, (d,))
    pu2[z] = pu1[...]

    def relay(step):
        up, down = lax.rem(z - step + 1 + NZ, NZ), lax.rem(z + step - 1, NZ)
        if step > 1:
            got(pu2.at[up], s_u2, (step - 2,))
            got(pu2.at[down], s_u2, (step + 2,))
        put(pu2.at[up], pu2.at[up], s_u2, (step - 1,), pz(1))
        if step < 4:
            put(pu2.at[down], pu2.at[down], s_u2, (step + 3,), pz(-1))

    relay(1)
    for i, d in enumerate((1, -1, far)):
        got(pt.at[others, ranks(c, y - d)], s_py, (i,))
        put(pt.at[others, ranks(c, y - d)], pt.at[others, ranks(c, y - d)], s_pc, (i,), py(0, True))
    relay(2)
    for i, d in enumerate((1, -1, -far, 0)):
        got(pt.at[others, ranks(o, y - d)], s_pc, (i,))
    own_t.wait()

    def send_cot():
        for k in range(CHUNKS):
            for d in (2, 1, 3):
                rows = pl.ds(lax.rem(x + d, NX) * QUARTER + STARTS[k], SIZES[k])
                put(cot.at[rows], c4.at[d, pl.ds(STARTS[k], SIZES[k])], s_c, (k, d), px(d))

    def at(d):
        return lax.rem(z + d + NZ, NZ)

    def sign(k):
        return 1 if k % 2 == 0 else -1

    def partial(k):
        rows = pl.ds(STARTS[k], SIZES[k])
        for d in (1, 3, 2):
            got(t4.at[d, rows], s_t, (k, d))
        low = None
        for d in range(NX):
            part = lax.dot_general(
                pt[d], t4[d, rows], (((1,), (1,)), ((), ())), preferred_element_type=F32
            )
            low = part if low is None else low + part
        psend[k][...] = low.astype(BF16).reshape(NZ, RANK // NZ, SIZES[k])
        e = sign(k)
        for owner, to, slot in ((-4, -e, 0), (-2 * e, e, 1), (e, -e, 2), (3 * e, e, 3), (-e, -e, 5)):
            put(psend[k].at[at(owner)], zr[k].at[slot], s_z, (k, slot), pz(to))

    def middle(k):
        e = sign(k)
        for owner, one, two, slot in ((-3 * e, 0, 1, 6), (2 * e, 2, 3, 7)):
            got(zr[k].at[one], s_z, (k, one))
            got(zr[k].at[two], s_z, (k, two))
            both = zr[k][one].astype(F32) + zr[k][two].astype(F32)
            zq[k][slot - 6] = (psend[k][at(owner)].astype(F32) + both).astype(BF16)
            put(zq[k].at[slot - 6], zr[k].at[slot], s_z, (k, slot), pz(owner))

    def reduce(k):
        e = sign(k)
        total = psend[k][z].astype(F32)
        for slot in (5, 7, 6):
            got(zr[k].at[slot], s_z, (k, slot))
            total = total + zr[k][slot].astype(F32)
        ag[k][z] = total.astype(BF16)
        for d in (3 * e, -2 * e, e):
            put(ag[k].at[z], ag[k].at[z], s_a, (k, d % 8), pz(d))

    def arrived(k, d):
        got(ag[k].at[at(-d)], s_a, (k, d % 8))

    def forward(k):
        e = sign(k)
        for d in (-2 * e, 3 * e):
            arrived(k, d)
            for f in (e, -e):
                put(ag[k].at[at(-d)], ag[k].at[at(-d)], s_a, (k, (d + f) % 8), pz(f))

    def send_update_rows():
        got(pu2.at[lax.rem(z - 4 + NZ, NZ)], s_u2, (3,))
        for d in range(NY):
            for e in range(2):
                peer = lax.rem(y + d, NY) * 2 + (o if e else c)
                src = pu2.at[pl.ds(2 * lax.rem(peer, 4), 2), peer // 4]
                if d == 0 and e == 0:
                    pu3[:, dp] = pu2[pl.ds(2 * lax.rem(peer, 4), 2), peer // 4]
                else:
                    put(src, pu3.at[:, dp], s_u3, (d, e), py(d, e == 1))

    for k in range(CHUNKS + 3):
        if k < CHUNKS:
            partial(k)
        if k == CHUNKS - 2:
            send_cot()
        if 0 <= k - 1 < CHUNKS:
            middle(k - 1)
        if 0 <= k - 2 < CHUNKS:
            reduce(k - 2)
        if 0 <= k - 3 < CHUNKS:
            forward(k - 3)
        if k < 2:
            relay(k + 3)
        if k == 2:
            send_update_rows()

    own_c.wait()
    for k in range(CHUNKS):
        rows = pl.ds(STARTS[k], SIZES[k])
        e = sign(k)
        for d in (e, -e, 2 * e, -3 * e, 4):
            arrived(k, d)
        low = ag[k][...].reshape(RANK, SIZES[k])
        for d in (0, 1, 3, 2):
            if d:
                got(c4.at[d, rows], s_c, (k, d))
            part = jnp.dot(low, c4[d, rows], preferred_element_type=F32).reshape(NY, 2, 32, WIDTH)
            acc[d] = part if k == 0 else acc[d] + part

    halves = (0, 1)
    for h in halves:
        for d in (2, 1, 3, 0):
            gs[h, d] = acc[d, :, o, h * 16 : h * 16 + 16].astype(BF16)
            put(gs.at[h, d], gc.at[h, d], s_g, (h, d), py(0, True))

    def paired(h, d):
        got(gc.at[h, d], s_g, (h, d))
        return acc[d, :, c, h * 16 : h * 16 + 16] + gc[h, d].astype(F32)

    for h in halves:
        for d in (2, 1, 3):
            xs[h, d] = paired(h, d).astype(BF16)
            put(xs.at[h, d], xr.at[h, d], s_x, (h, d), px(-d))
    for h in halves:
        total = paired(h, 0)
        for d in (1, 3, 2):
            got(xr.at[h, d], s_x, (h, d))
            total = total + xr[h, d].astype(F32)
        ysum[h] = total
        ys[h] = total.astype(BF16)
        for d in (4, 3, 5, 2, 6, 1, 7):
            put(ys.at[h, lax.rem(y + d, NY)], yr.at[h, d], s_y, (h, d), py(d))
    for load in loads[1:]:
        load.wait()
    first_fix = 1.0 - BETA_ONE**STEP
    second_fix = 1.0 - BETA_TWO**STEP
    for h in halves:
        gradient = ysum[h, y]
        for d in (1, 7, 2, 6, 3, 5, 4):
            got(yr.at[h, d], s_y, (h, d))
            gradient = gradient + yr[h, d].astype(F32)
        rows = pl.ds(h * 16, 16)
        new_first = BETA_ONE * m1[rows] + (1.0 - BETA_ONE) * gradient
        new_second = BETA_TWO * m2[rows] + (1.0 - BETA_TWO) * gradient * gradient
        direction = new_first / first_fix / (jnp.sqrt(new_second / second_fix) + EPSILON)
        dirb[y, c, h] = direction.astype(BF16)
        for d in (4, 3, 5, 2, 6, 1, 7):
            put(dirb.at[y, c, h], dirb.at[y, c, h], s_d, (h, d), py(d))
        n1[rows] = new_first
        n2[rows] = new_second
    for d in range(NY):
        for e in range(2):
            if d or e:
                peer = lax.rem(y - d + NY, NY) * 2 + (o if e else c)
                got(pu3.at[:, peer], s_u3, (d, e))
    for h in halves:
        for d in (1, 7, 2, 6, 3, 5, 4):
            got(dirb.at[lax.rem(y - d + NY, NY), c, h], s_d, (h, d))
        put(dirb.at[:, c, h], dirb.at[:, c, h], s_dc, (h,), py(0, True))
    for h in halves:
        got(dirb.at[:, o, h], s_dc, (h,))
    update = jnp.dot(
        pu3[...].reshape(RANK, RANK), dirb[...].reshape(RANK, WIDTH), preferred_element_type=F32
    )
    nw[...] = (wgt[...].astype(F32) - RATE * update).astype(BF16)
    for cp in sent:
        cp.wait_send()


def hand_over(nw, n1, n2, nw_out, n1_out, n2_out, a, b, e, sems):
    trips = ((nw, a, nw_out), (n1, b, n1_out), (n2, e, n2_out))
    ins = [pltpu.make_async_copy(src, mid, sems.at[0, i]) for i, (src, mid, _) in enumerate(trips)]
    outs = [pltpu.make_async_copy(mid, dst, sems.at[1, i]) for i, (_, mid, dst) in enumerate(trips)]
    for copy in ins:
        copy.start()
    for first, second in zip(ins, outs):
        first.wait()
        second.start()
    for copy in outs:
        copy.wait()


def shards(tokens, cotangent, projection, weight, first_moment, second_moment):
    vmem = pl.BlockSpec(memory_space=pltpu.VMEM)
    hbm = pl.BlockSpec(memory_space=pltpu.HBM)
    dma = pltpu.SemaphoreType.DMA
    v = pltpu.VMEM

    def pair(*n):
        return dma(n), dma(n)

    scratch = [
        v(projection.shape, BF16),
        v(weight.shape, BF16),
        v(first_moment.shape, F32),
        v(second_moment.shape, F32),
        v((NX, RANK, WIDTH), BF16),
        v((NX, QUARTER, WIDTH), BF16),
        v((NX, QUARTER, WIDTH), BF16),
        tuple(v((NZ, RANK // NZ, n), BF16) for n in SIZES),
        tuple(v((NZ, RANK // NZ, n), BF16) for n in SIZES),
        tuple(v((2, RANK // NZ, n), BF16) for n in SIZES),
        tuple(v((NZ, RANK // NZ, n), BF16) for n in SIZES),
        v((NX, NY, 2, 32, WIDTH), F32),
        v((2, NX, NY, 16, WIDTH), BF16),
        v((2, NX, NY, 16, WIDTH), BF16),
        v((2, NX, NY, 16, WIDTH), BF16),
        v((2, NX, NY, 16, WIDTH), BF16),
        v((2, NY, 16, WIDTH), F32),
        v((2, NY, 16, WIDTH), BF16),
        v((2, NY, 16, WIDTH), BF16),
        v((NY, 2, 2, 16, WIDTH), BF16),
        v((NX, 16, RANK), BF16),
        v((NZ, NX, 16, RANK), BF16),
        v((2, 16, 16, RANK), BF16),
        dma((6,)),
        pair(NX), pair(3), pair(4),
        pair(CHUNKS, NX), pair(CHUNKS, NX), pair(CHUNKS, NZ), pair(CHUNKS, NZ),
        pair(2, NX), pair(2, NX), pair(2, NY), pair(2, NY), pair(2),
        pair(NX), pair(7), pair(NY, 2),
    ]
    shapes = (
        jax.ShapeDtypeStruct(weight.shape, weight.dtype),
        jax.ShapeDtypeStruct(first_moment.shape, F32),
        jax.ShapeDtypeStruct(second_moment.shape, F32),
    )
    results = pl.pallas_call(
        kernel,
        out_shape=shapes,
        in_specs=[hbm] * 6,
        out_specs=(vmem, vmem, vmem),
        scratch_shapes=scratch,
        compiler_params=pltpu.CompilerParams(
            collective_id=0, has_side_effects=True, vmem_limit_bytes=63 * 2**20
        ),
        cost_estimate=pl.CostEstimate(flops=1_800_000_000, bytes_accessed=4_500_000, transcendentals=8192),
    )(tokens, cotangent, projection, weight, first_moment, second_moment)
    return pl.pallas_call(
        hand_over,
        out_shape=shapes,
        in_specs=[hbm] * 3,
        out_specs=(hbm, hbm, hbm),
        scratch_shapes=[v(t.shape, t.dtype) for t in shapes] + [dma((2, 3))],
        compiler_params=pltpu.CompilerParams(vmem_limit_bytes=63 * 2**20),
    )(*results)


def solution(mesh):
    return jax.shard_map(
        shards,
        mesh=mesh,
        in_specs=(
            P("dp", "fsdp"),
            P("dp", "fsdp"),
            P("fsdp", None),
            P("dp", "fsdp"),
            P("dp", "fsdp"),
            P("dp", "fsdp"),
        ),
        out_specs=(P("dp", "fsdp"), P("dp", "fsdp"), P("dp", "fsdp")),
        check_vma=False,
    )
```

```python
import functools

import jax
import jax.numpy as jnp
from jax import lax
from jax.experimental import pallas as pl
from jax.experimental.pallas import tpu as pltpu
from jax.sharding import PartitionSpec as P

STEP = 10
BETA_ONE = 0.9
BETA_TWO = 0.999
EPSILON = 1e-08
RATE = 0.1

NX, NY, NZ = 4, 8, 8
RANK = 512
WIDTH = 256
QUARTER = 768
SIZES = (256, 256, 256)
CHUNKS = len(SIZES)
STARTS = tuple(sum(SIZES[:k]) for k in range(CHUNKS))
MESH = pl.DeviceIdType.MESH
F32 = jnp.float32
BF16 = jnp.bfloat16


def kernel(
    tok, cot, proj_hbm, wgt_hbm, m1_hbm, m2_hbm, nw, n1, n2,
    proj, wgt, m1, m2, pt, t4, c4, psend, zr, zq, ag, acc, gs, gc, xs, xr, ysum, ys, yr, dirb,
    pu1, pu2, pu3, y2sum, y2s, y2r, x2s, x2r,
    lsem, s_out, s_pt, s_py, s_pc, s_t, s_c, s_z, s_a, s_g, s_x, s_y, s_y2, s_x2, s_d, s_dc, s_u1, s_u2, s_u3,
):
    dp = lax.axis_index("dp")
    fs = lax.axis_index("fsdp")
    y, c = dp // 2, lax.rem(dp, 2)
    x, z = fs // NZ, lax.rem(fs, NZ)
    o = 1 - c

    def px(d):
        return (dp, lax.rem(x + d + NX, NX) * NZ + z)

    def pz(d):
        return (dp, x * NZ + lax.rem(z + d + NZ, NZ))

    def py(d, other=False):
        return (lax.rem(y + d + NY, NY) * 2 + (o if other else c), fs)

    sent = []

    def put(src, dst, sem, dev):
        cp = pltpu.make_async_remote_copy(
            src_ref=src, dst_ref=dst, send_sem=s_out, recv_sem=sem, device_id=dev, device_id_type=MESH
        )
        cp.start()
        sent.append(cp)

    def got(dst, sem):
        pltpu.make_async_remote_copy(
            src_ref=dst, dst_ref=dst, send_sem=s_out, recv_sem=sem, device_id=(dp, fs), device_id_type=MESH
        ).wait_recv()

    own_t = pltpu.make_async_copy(tok.at[pl.ds(x * QUARTER, QUARTER)], t4.at[0], lsem.at[0])
    own_c = pltpu.make_async_copy(cot.at[pl.ds(x * QUARTER, QUARTER)], c4.at[0], lsem.at[1])
    loads = [
        pltpu.make_async_copy(src, dst, lsem.at[i + 2])
        for i, (src, dst) in enumerate(((proj_hbm, proj), (wgt_hbm, wgt), (m1_hbm, m1), (m2_hbm, m2)))
    ]
    for load in loads:
        load.start()
    own_t.start()
    own_c.start()

    barrier = pltpu.get_barrier_semaphore()
    for d in range(1, NX):
        pl.semaphore_signal(barrier, inc=1, device_id=px(d), device_id_type=MESH)
    for d in range(1, NZ):
        pl.semaphore_signal(barrier, inc=1, device_id=pz(d), device_id_type=MESH)
    for d in range(NY):
        pl.semaphore_signal(barrier, inc=1, device_id=py(d, True), device_id_type=MESH)
        if d:
            pl.semaphore_signal(barrier, inc=1, device_id=py(d), device_id_type=MESH)
    loads[0].wait()
    pt[0] = proj[...].T
    pu1[x] = proj[pl.ds(dp * 16, 16)]
    pl.semaphore_wait(barrier, NX - 1 + NZ - 1 + 2 * NY - 1)

    def ranks(core, row):
        return pl.ds(core * 256 + lax.rem(row + NY, 4) * 64, 64)

    others = pl.ds(1, NX - 1)
    for d in (2, 1, 3):
        put(pt.at[0, ranks(c, y)], pt.at[d, ranks(c, y)], s_pt.at[0], px(d))
    for d in (2, 1, 3):
        put(pu1.at[x], pu1.at[x], s_u1.at[0], px(d))
    for k in range(CHUNKS):
        for d in (2, 1, 3):
            rows = pl.ds(lax.rem(x + d, NX) * QUARTER + STARTS[k], SIZES[k])
            put(tok.at[rows], t4.at[d, pl.ds(STARTS[k], SIZES[k])], s_t.at[k], px(d))

    got(pt.at[others, ranks(c, y)], s_pt.at[0])
    far = 2 - 4 * c
    for i, d in enumerate((1, -1, far)):
        put(pt.at[others, ranks(c, y)], pt.at[others, ranks(c, y)], s_py.at[i], py(d))
    put(pt.at[others, ranks(c, y)], pt.at[others, ranks(c, y)], s_pc.at[0], py(0, True))

    got(pu1.at[others], s_u1.at[0])
    pu2[z] = pu1[...]

    def relay(step):
        up, down = lax.rem(z - step + 1 + NZ, NZ), lax.rem(z + step - 1, NZ)
        if step > 1:
            got(pu2.at[up], s_u2.at[step - 2])
            got(pu2.at[down], s_u2.at[step + 2])
        put(pu2.at[up], pu2.at[up], s_u2.at[step - 1], pz(1))
        if step < 4:
            put(pu2.at[down], pu2.at[down], s_u2.at[step + 3], pz(-1))

    relay(1)
    for i, d in enumerate((1, -1, far)):
        got(pt.at[others, ranks(c, y - d)], s_py.at[i])
        put(pt.at[others, ranks(c, y - d)], pt.at[others, ranks(c, y - d)], s_pc.at[0], py(0, True))
    relay(2)
    got(pt.at[others, pl.ds(o * 256, 256)], s_pc.at[0])
    own_t.wait()

    def send_cot():
        for k in range(CHUNKS):
            for d in (2, 1, 3):
                rows = pl.ds(lax.rem(x + d, NX) * QUARTER + STARTS[k], SIZES[k])
                put(cot.at[rows], c4.at[d, pl.ds(STARTS[k], SIZES[k])], s_c.at[k], px(d))

    def at(d):
        return lax.rem(z + d + NZ, NZ)

    def sign(k):
        return 1 if k % 2 == 0 else -1

    def partial(k):
        rows = pl.ds(STARTS[k], SIZES[k])
        got(t4.at[others, rows], s_t.at[k])
        low = None
        for d in range(NX):
            part = lax.dot_general(
                pt[d], t4[d, rows], (((1,), (1,)), ((), ())), preferred_element_type=F32
            )
            low = part if low is None else low + part
        psend[k][...] = low.astype(BF16).reshape(NZ, RANK // NZ, SIZES[k])
        e = sign(k)
        for owner, to, slot in ((-4, -e, 0), (-2 * e, e, 1), (e, -e, 2), (3 * e, e, 3), (-e, -e, 4)):
            put(psend[k].at[at(owner)], zr[k].at[slot], s_z.at[k, slot // 4], pz(to))

    def middle(k):
        e = sign(k)
        got(zr[k].at[pl.ds(0, 4)], s_z.at[k, 0])
        for owner, one, two, slot in ((-3 * e, 0, 1, 5), (2 * e, 2, 3, 6)):
            both = zr[k][one].astype(F32) + zr[k][two].astype(F32)
            zq[k][slot - 5] = (psend[k][at(owner)].astype(F32) + both).astype(BF16)
            put(zq[k].at[slot - 5], zr[k].at[slot], s_z.at[k, 1], pz(owner))

    def reduce(k):
        e = sign(k)
        total = psend[k][z].astype(F32)
        got(zr[k].at[pl.ds(4, 3)], s_z.at[k, 1])
        for slot in (4, 5, 6):
            total = total + zr[k][slot].astype(F32)
        ag[k][z] = total.astype(BF16)
        for d in (3 * e, -2 * e, e):
            put(ag[k].at[z], ag[k].at[z], s_a.at[k, 1 if d == e else 0], pz(d))

    def forward(k):
        e = sign(k)
        got(ag[k].at[pl.ds(0, 2)], s_a.at[k, 0])
        for d in (-2 * e, 3 * e):
            for f in (e, -e):
                put(ag[k].at[at(-d)], ag[k].at[at(-d)], s_a.at[k, 1], pz(f))

    def send_update_rows():
        got(pu2.at[lax.rem(z - 4 + NZ, NZ)], s_u2.at[3])
        for d in range(NY):
            for e in range(2):
                peer = lax.rem(y + d, NY) * 2 + (o if e else c)
                src = pu2.at[pl.ds(2 * lax.rem(peer, 4), 2), peer // 4]
                if d == 0 and e == 0:
                    pu3[:, dp] = pu2[pl.ds(2 * lax.rem(peer, 4), 2), peer // 4]
                else:
                    put(src, pu3.at[:, dp], s_u3.at[0], py(d, e == 1))

    for k in range(CHUNKS + 3):
        if k < CHUNKS:
            partial(k)
        if k == CHUNKS - 2:
            send_cot()
        if 0 <= k - 1 < CHUNKS:
            middle(k - 1)
        if 0 <= k - 2 < CHUNKS:
            reduce(k - 2)
        if 0 <= k - 3 < CHUNKS:
            forward(k - 3)
        if k < 2:
            relay(k + 3)
        if k == 2:
            send_update_rows()

    own_c.wait()
    for k in range(CHUNKS):
        rows = pl.ds(STARTS[k], SIZES[k])
        got(ag[k].at[pl.ds(0, 5)], s_a.at[k, 1])
        got(c4.at[others, rows], s_c.at[k])
        low = ag[k][...].reshape(RANK, SIZES[k])
        for d in (2, 1, 3, 0):
            part = jnp.dot(low, c4[d, rows], preferred_element_type=F32).reshape(NY, 2, 32, WIDTH)
            acc[d] = part if k == 0 else acc[d] + part

    halves = (0, 1)
    order = (2, 1, 3, 0)
    groups = (pl.ds(0, 1), pl.ds(1, 2), pl.ds(3, 1))
    for h in halves:
        for i, group in enumerate(groups):
            for slot in range(group.start, group.start + group.size):
                gs[h, slot] = acc[order[slot], :, o, h * 16 : h * 16 + 16].astype(BF16)
            put(gs.at[h, group], gc.at[h, group], s_g.at[h, i], py(0, True))

    def paired(h, slot):
        return acc[order[slot], :, c, h * 16 : h * 16 + 16] + gc[h, slot].astype(F32)

    for h in halves:
        got(gc.at[h, groups[0]], s_g.at[h, 0])
        total = paired(h, 0)
        y2sum[h] = total
        y2s[h] = total.astype(BF16)
        for d in (4, 3, 5, 2, 6, 1, 7):
            put(y2s.at[h, lax.rem(y + d, NY)], y2r.at[h, d], s_y2.at[h], py(d))
        got(gc.at[h, groups[1]], s_g.at[h, 1])
        for slot in (1, 2):
            xs[h, slot - 1] = paired(h, slot).astype(BF16)
            put(xs.at[h, slot - 1], xr.at[h, slot - 1], s_x.at[h], px(-order[slot]))
    for h in halves:
        got(gc.at[h, groups[2]], s_g.at[h, 2])
        total = paired(h, 3)
        got(xr.at[h], s_x.at[h])
        total = total + xr[h, 0].astype(F32) + xr[h, 1].astype(F32)
        ysum[h] = total
        ys[h] = total.astype(BF16)
        for d in (4, 3, 5, 2, 6, 1, 7):
            put(ys.at[h, lax.rem(y + d, NY)], yr.at[h, d], s_y.at[h], py(d))
    for h in halves:
        got(y2r.at[h, pl.ds(1, NY - 1)], s_y2.at[h])
        total = y2sum[h, y]
        for d in range(1, NY):
            total = total + y2r[h, d].astype(F32)
        x2s[h] = total.astype(BF16)
        put(x2s.at[h], x2r.at[h], s_x2.at[h], px(2))
    for load in loads[1:]:
        load.wait()
    first_fix = 1.0 - BETA_ONE**STEP
    second_fix = 1.0 - BETA_TWO**STEP
    for h in halves:
        got(yr.at[h, pl.ds(1, NY - 1)], s_y.at[h])
        got(x2r.at[h], s_x2.at[h])
        gradient = ysum[h, y] + x2r[h].astype(F32)
        for d in range(1, NY):
            gradient = gradient + yr[h, d].astype(F32)
        rows = pl.ds(h * 16, 16)
        new_first = BETA_ONE * m1[rows] + (1.0 - BETA_ONE) * gradient
        new_second = BETA_TWO * m2[rows] + (1.0 - BETA_TWO) * gradient * gradient
        direction = new_first / first_fix / (jnp.sqrt(new_second / second_fix) + EPSILON)
        dirb[y, c, h] = direction.astype(BF16)
        for d in (4, 3, 5, 2, 6, 1, 7):
            put(dirb.at[y, c, h], dirb.at[y, c, h], s_d.at[h], py(d))
        n1[rows] = new_first
        n2[rows] = new_second
    got(pu3.at[:, pl.ds(0, 2 * NY - 1)], s_u3.at[0])
    for h in halves:
        got(dirb.at[pl.ds(0, NY - 1), c, h], s_d.at[h])
        put(dirb.at[:, c, h], dirb.at[:, c, h], s_dc.at[h], py(0, True))
    for h in halves:
        got(dirb.at[:, o, h], s_dc.at[h])
    update = jnp.dot(
        pu3[...].reshape(RANK, RANK), dirb[...].reshape(RANK, WIDTH), preferred_element_type=F32
    )
    nw[...] = (wgt[...].astype(F32) - RATE * update).astype(BF16)
    for cp in sent:
        cp.wait_send()


def hand_over(nw, n1, n2, nw_out, n1_out, n2_out, a, b, e, sems):
    trips = ((nw, a, nw_out), (n1, b, n1_out), (n2, e, n2_out))
    ins = [pltpu.make_async_copy(src, mid, sems.at[0, i]) for i, (src, mid, _) in enumerate(trips)]
    outs = [pltpu.make_async_copy(mid, dst, sems.at[1, i]) for i, (_, mid, dst) in enumerate(trips)]
    for copy in ins:
        copy.start()
    for first, second in zip(ins, outs):
        first.wait()
        second.start()
    for copy in outs:
        copy.wait()


def shards(tokens, cotangent, projection, weight, first_moment, second_moment):
    vmem = pl.BlockSpec(memory_space=pltpu.VMEM)
    hbm = pl.BlockSpec(memory_space=pltpu.HBM)
    dma = pltpu.SemaphoreType.DMA
    v = pltpu.VMEM
    scratch = [
        v(projection.shape, BF16),
        v(weight.shape, BF16),
        v(first_moment.shape, F32),
        v(second_moment.shape, F32),
        v((NX, RANK, WIDTH), BF16),
        v((NX, QUARTER, WIDTH), BF16),
        v((NX, QUARTER, WIDTH), BF16),
        tuple(v((NZ, RANK // NZ, n), BF16) for n in SIZES),
        tuple(v((NZ, RANK // NZ, n), BF16) for n in SIZES),
        tuple(v((2, RANK // NZ, n), BF16) for n in SIZES),
        tuple(v((NZ, RANK // NZ, n), BF16) for n in SIZES),
        v((NX, NY, 2, 32, WIDTH), F32),
        v((2, NX, NY, 16, WIDTH), BF16),
        v((2, NX, NY, 16, WIDTH), BF16),
        v((2, 2, NY, 16, WIDTH), BF16),
        v((2, 2, NY, 16, WIDTH), BF16),
        v((2, NY, 16, WIDTH), F32),
        v((2, NY, 16, WIDTH), BF16),
        v((2, NY, 16, WIDTH), BF16),
        v((NY, 2, 2, 16, WIDTH), BF16),
        v((NX, 16, RANK), BF16),
        v((NZ, NX, 16, RANK), BF16),
        v((2, 16, 16, RANK), BF16),
        v((2, NY, 16, WIDTH), F32),
        v((2, NY, 16, WIDTH), BF16),
        v((2, NY, 16, WIDTH), BF16),
        v((2, 16, WIDTH), BF16),
        v((2, 16, WIDTH), BF16),
        dma((6,)), dma(()),
        dma((1,)), dma((3,)), dma((1,)),
        dma((CHUNKS,)), dma((CHUNKS,)), dma((CHUNKS, 2)), dma((CHUNKS, 2)),
        dma((2, 3)), dma((2,)), dma((2,)), dma((2,)), dma((2,)), dma((2,)), dma((2,)),
        dma((1,)), dma((7,)), dma((1,)),
    ]
    shapes = (
        jax.ShapeDtypeStruct(weight.shape, weight.dtype),
        jax.ShapeDtypeStruct(first_moment.shape, F32),
        jax.ShapeDtypeStruct(second_moment.shape, F32),
    )
    results = pl.pallas_call(
        kernel,
        out_shape=shapes,
        in_specs=[hbm] * 6,
        out_specs=(vmem, vmem, vmem),
        scratch_shapes=scratch,
        compiler_params=pltpu.CompilerParams(
            collective_id=0, has_side_effects=True, vmem_limit_bytes=63 * 2**20
        ),
        cost_estimate=pl.CostEstimate(flops=1_800_000_000, bytes_accessed=4_500_000, transcendentals=8192),
    )(tokens, cotangent, projection, weight, first_moment, second_moment)
    return pl.pallas_call(
        hand_over,
        out_shape=shapes,
        in_specs=[hbm] * 3,
        out_specs=(hbm, hbm, hbm),
        scratch_shapes=[v(t.shape, t.dtype) for t in shapes] + [dma((2, 3))],
        compiler_params=pltpu.CompilerParams(vmem_limit_bytes=63 * 2**20),
    )(*results)


def solution(mesh):
    return jax.shard_map(
        shards,
        mesh=mesh,
        in_specs=(
            P("dp", "fsdp"),
            P("dp", "fsdp"),
            P("fsdp", None),
            P("dp", "fsdp"),
            P("dp", "fsdp"),
            P("dp", "fsdp"),
        ),
        out_specs=(P("dp", "fsdp"), P("dp", "fsdp"), P("dp", "fsdp")),
        check_vma=False,
    )
```

```python
import functools

import jax
import jax.numpy as jnp
from jax import lax
from jax.experimental import pallas as pl
from jax.experimental.pallas import tpu as pltpu
from jax.sharding import PartitionSpec as P

STEP = 10
BETA_ONE = 0.9
BETA_TWO = 0.999
EPSILON = 1e-08
RATE = 0.1

NX, NY, NZ = 4, 8, 8
RANK = 512
WIDTH = 256
QUARTER = 768
SIZES = (128, 256, 256, 128)
CHUNKS = len(SIZES)
STARTS = tuple(sum(SIZES[:k]) for k in range(CHUNKS))
MESH = pl.DeviceIdType.MESH
F32 = jnp.float32
BF16 = jnp.bfloat16


def kernel(
    tok, cot, proj_hbm, wgt_hbm, m1_hbm, m2_hbm, nw, n1, n2,
    proj, wgt, m1, m2, pt, t4, c4, psend, zr, zq, ag, acc, gs, gc, xs, xr, ysum, ys, yr, dirb,
    pu1, pu2, pu3, y2sum, y2s, y2r, x2s, x2r,
    lsem, s_out, s_pt, s_py, s_pc, s_t, s_c, s_z, s_a, s_g, s_x, s_y, s_y2, s_x2, s_d, s_dc, s_u1, s_u2, s_u3,
):
    dp = lax.axis_index("dp")
    fs = lax.axis_index("fsdp")
    y, c = dp // 2, lax.rem(dp, 2)
    x, z = fs // NZ, lax.rem(fs, NZ)
    o = 1 - c

    def px(d):
        return (dp, lax.rem(x + d + NX, NX) * NZ + z)

    def pz(d):
        return (dp, x * NZ + lax.rem(z + d + NZ, NZ))

    def py(d, other=False):
        return (lax.rem(y + d + NY, NY) * 2 + (o if other else c), fs)

    sent = []

    def put(src, dst, sem, dev):
        cp = pltpu.make_async_remote_copy(
            src_ref=src, dst_ref=dst, send_sem=s_out, recv_sem=sem, device_id=dev, device_id_type=MESH
        )
        cp.start()
        sent.append(cp)

    def drain(keep=0):
        while len(sent) > keep:
            sent.pop(0).wait_send()

    def got(dst, sem):
        pltpu.make_async_remote_copy(
            src_ref=dst, dst_ref=dst, send_sem=s_out, recv_sem=sem, device_id=(dp, fs), device_id_type=MESH
        ).wait_recv()

    barrier = pltpu.get_barrier_semaphore()
    for d in range(1, NX):
        pl.semaphore_signal(barrier, inc=1, device_id=px(d), device_id_type=MESH)
    for d in range(1, NZ):
        pl.semaphore_signal(barrier, inc=1, device_id=pz(d), device_id_type=MESH)
    for d in range(NY):
        pl.semaphore_signal(barrier, inc=1, device_id=py(d, True), device_id_type=MESH)
        if d:
            pl.semaphore_signal(barrier, inc=1, device_id=py(d), device_id_type=MESH)
    own_t = pltpu.make_async_copy(tok.at[x], t4.at[0], lsem.at[0])
    own_c = pltpu.make_async_copy(cot.at[x], c4.at[0], lsem.at[1])
    loads = [
        pltpu.make_async_copy(src, dst, lsem.at[i + 2])
        for i, (src, dst) in enumerate(((proj_hbm, proj), (wgt_hbm, wgt), (m1_hbm, m1), (m2_hbm, m2)))
    ]
    for load in loads:
        load.start()
    own_t.start()
    own_c.start()

    def send_tok(k):
        rows = pl.ds(STARTS[k], SIZES[k])
        for d in (2, 1, 3):
            put(tok.at[lax.rem(x + d, NX), rows], t4.at[d, rows], s_t.at[k], px(d))

    loads[0].wait()
    pt[0] = proj[...].T
    pu1[x] = proj[pl.ds(dp * 16, 16)]
    pl.semaphore_wait(barrier, NX - 1 + NZ - 1 + 2 * NY - 1)

    def ranks(core, row):
        return pl.ds(core * 256 + lax.rem(row + NY, 4) * 64, 64)

    others = pl.ds(1, NX - 1)
    for d in (2, 1, 3):
        put(pt.at[0, ranks(c, y)], pt.at[d, ranks(c, y)], s_pt.at[0], px(d))
    for d in (2, 1, 3):
        put(pu1.at[x], pu1.at[x], s_u1.at[0], px(d))
    for k in range(CHUNKS):
        send_tok(k)

    got(pt.at[others, ranks(c, y)], s_pt.at[0])
    far = 2 - 4 * c
    for i, d in enumerate((1, -1, far)):
        put(pt.at[others, ranks(c, y)], pt.at[others, ranks(c, y)], s_py.at[i], py(d))
    put(pt.at[others, ranks(c, y)], pt.at[others, ranks(c, y)], s_pc.at[0], py(0, True))

    got(pu1.at[others], s_u1.at[0])
    pu2[z] = pu1[...]

    def relay(step):
        up, down = lax.rem(z - step + 1 + NZ, NZ), lax.rem(z + step - 1, NZ)
        if step > 1:
            got(pu2.at[up], s_u2.at[step - 2])
            got(pu2.at[down], s_u2.at[step + 2])
        put(pu2.at[up], pu2.at[up], s_u2.at[step - 1], pz(1))
        if step < 4:
            put(pu2.at[down], pu2.at[down], s_u2.at[step + 3], pz(-1))

    relay(1)
    for i, d in enumerate((1, -1, far)):
        got(pt.at[others, ranks(c, y - d)], s_py.at[i])
        put(pt.at[others, ranks(c, y - d)], pt.at[others, ranks(c, y - d)], s_pc.at[0], py(0, True))
    relay(2)
    got(pt.at[others, pl.ds(o * 256, 256)], s_pc.at[0])
    own_t.wait()

    def send_cot():
        for k in range(CHUNKS):
            for d in (2, 1, 3):
                rows = pl.ds(STARTS[k], SIZES[k])
                put(cot.at[lax.rem(x + d, NX), rows], c4.at[d, rows], s_c.at[k], px(d))

    def at(d):
        return lax.rem(z + d + NZ, NZ)

    def sign(k):
        return 1 if k % 2 == 0 else -1

    def partial(k):
        rows = pl.ds(STARTS[k], SIZES[k])
        got(t4.at[others, rows], s_t.at[k])
        low = None
        for d in range(NX):
            part = lax.dot_general(
                pt[d], t4[d, rows], (((1,), (1,)), ((), ())), preferred_element_type=F32
            )
            low = part if low is None else low + part
        psend[k][...] = low.astype(BF16).reshape(NZ, RANK // NZ, SIZES[k])
        e = sign(k)
        for owner, to, slot in ((-4, -e, 0), (-2 * e, e, 1), (e, -e, 2), (3 * e, e, 3), (-e, -e, 4)):
            put(psend[k].at[at(owner)], zr[k].at[slot], s_z.at[k, slot // 4], pz(to))

    def middle(k):
        e = sign(k)
        got(zr[k].at[pl.ds(0, 4)], s_z.at[k, 0])
        for owner, one, two, slot in ((-3 * e, 0, 1, 5), (2 * e, 2, 3, 6)):
            both = zr[k][one].astype(F32) + zr[k][two].astype(F32)
            zq[k][slot - 5] = (psend[k][at(owner)].astype(F32) + both).astype(BF16)
            put(zq[k].at[slot - 5], zr[k].at[slot], s_z.at[k, 1], pz(owner))

    def reduce(k):
        e = sign(k)
        total = psend[k][z].astype(F32)
        got(zr[k].at[pl.ds(4, 3)], s_z.at[k, 1])
        for slot in (4, 5, 6):
            total = total + zr[k][slot].astype(F32)
        ag[k][z] = total.astype(BF16)
        for d in (3 * e, -2 * e, e):
            put(ag[k].at[z], ag[k].at[z], s_a.at[k, 1 if d == e else 0], pz(d))

    def forward(k):
        e = sign(k)
        got(ag[k].at[pl.ds(0, 2)], s_a.at[k, 0])
        for d in (-2 * e, 3 * e):
            for f in (e, -e):
                put(ag[k].at[at(-d)], ag[k].at[at(-d)], s_a.at[k, 1], pz(f))

    def send_update_rows():
        got(pu2.at[lax.rem(z - 4 + NZ, NZ)], s_u2.at[3])
        for d in range(NY):
            for e in range(2):
                peer = lax.rem(y + d, NY) * 2 + (o if e else c)
                src = pu2.at[pl.ds(2 * lax.rem(peer, 4), 2), peer // 4]
                if d == 0 and e == 0:
                    pu3[:, dp] = pu2[pl.ds(2 * lax.rem(peer, 4), 2), peer // 4]
                else:
                    put(src, pu3.at[:, dp], s_u3.at[0], py(d, e == 1))

    for k in range(CHUNKS + 3):
        if k < CHUNKS:
            partial(k)
        if k == CHUNKS - 2:
            send_cot()
        if 0 <= k - 1 < CHUNKS:
            middle(k - 1)
        if 0 <= k - 2 < CHUNKS:
            reduce(k - 2)
        if 0 <= k - 3 < CHUNKS:
            forward(k - 3)
        if k < 2:
            relay(k + 3)
        if k == 2:
            send_update_rows()

    own_c.wait()
    for k in range(CHUNKS):
        rows = pl.ds(STARTS[k], SIZES[k])
        got(ag[k].at[pl.ds(0, 5)], s_a.at[k, 1])
        if k == CHUNKS - 1:
            drain(3 * CHUNKS)
        got(c4.at[others, rows], s_c.at[k])
        low = ag[k][...].reshape(RANK, SIZES[k])
        for d in (2, 1, 3, 0):
            part = jnp.dot(low, c4[d, rows], preferred_element_type=F32).reshape(NY, 2, 32, WIDTH)
            acc[d] = part if k == 0 else acc[d] + part

    halves = (0, 1)
    order = (2, 1, 3, 0)
    groups = (pl.ds(0, 1), pl.ds(1, 2), pl.ds(3, 1))
    for h in halves:
        for i, group in enumerate(groups):
            for slot in range(group.start, group.start + group.size):
                gs[h, slot] = acc[order[slot], :, o, h * 16 : h * 16 + 16].astype(BF16)
            put(gs.at[h, group], gc.at[h, group], s_g.at[h, i], py(0, True))

    def paired(h, slot):
        return acc[order[slot], :, c, h * 16 : h * 16 + 16] + gc[h, slot].astype(F32)

    for h in halves:
        got(gc.at[h, groups[0]], s_g.at[h, 0])
        total = paired(h, 0)
        y2sum[h] = total
        y2s[h] = total.astype(BF16)
        for d in (4, 3, 5, 2, 6, 1, 7):
            put(y2s.at[h, lax.rem(y + d, NY)], y2r.at[h, d], s_y2.at[h], py(d))
        got(gc.at[h, groups[1]], s_g.at[h, 1])
        for slot in (1, 2):
            xs[h, slot - 1] = paired(h, slot).astype(BF16)
            put(xs.at[h, slot - 1], xr.at[h, slot - 1], s_x.at[h], px(-order[slot]))
    drain(22)
    for h in halves:
        got(gc.at[h, groups[2]], s_g.at[h, 2])
        total = paired(h, 3)
        got(xr.at[h], s_x.at[h])
        total = total + xr[h, 0].astype(F32) + xr[h, 1].astype(F32)
        ysum[h] = total
        ys[h] = total.astype(BF16)
        for d in (4, 3, 5, 2, 6, 1, 7):
            put(ys.at[h, lax.rem(y + d, NY)], yr.at[h, d], s_y.at[h], py(d))
    drain(14)
    for h in halves:
        got(y2r.at[h, pl.ds(1, NY - 1)], s_y2.at[h])
        total = y2sum[h, y]
        for d in range(1, NY):
            total = total + y2r[h, d].astype(F32)
        x2s[h] = total.astype(BF16)
        put(x2s.at[h], x2r.at[h], s_x2.at[h], px(2))
    for load in loads[1:]:
        load.wait()
    first_fix = 1.0 - BETA_ONE**STEP
    second_fix = 1.0 - BETA_TWO**STEP
    for h in halves:
        got(yr.at[h, pl.ds(1, NY - 1)], s_y.at[h])
        got(x2r.at[h], s_x2.at[h])
        gradient = ysum[h, y] + x2r[h].astype(F32)
        for d in range(1, NY):
            gradient = gradient + yr[h, d].astype(F32)
        rows = pl.ds(h * 16, 16)
        new_first = BETA_ONE * m1[rows] + (1.0 - BETA_ONE) * gradient
        new_second = BETA_TWO * m2[rows] + (1.0 - BETA_TWO) * gradient * gradient
        direction = new_first / first_fix / (jnp.sqrt(new_second / second_fix) + EPSILON)
        dirb[y, c, h] = direction.astype(BF16)
        for d in (4, 3, 5, 2, 6, 1, 7):
            put(dirb.at[y, c, h], dirb.at[y, c, h], s_d.at[h], py(d))
        n1[rows] = new_first
        n2[rows] = new_second
    drain(14)
    got(pu3.at[:, pl.ds(0, 2 * NY - 1)], s_u3.at[0])
    for h in halves:
        got(dirb.at[pl.ds(0, NY - 1), c, h], s_d.at[h])
        put(dirb.at[:, c, h], dirb.at[:, c, h], s_dc.at[h], py(0, True))
    for h in halves:
        got(dirb.at[:, o, h], s_dc.at[h])
    update = jnp.dot(
        pu3[...].reshape(RANK, RANK), dirb[...].reshape(RANK, WIDTH), preferred_element_type=F32
    )
    nw[...] = (wgt[...].astype(F32) - RATE * update).astype(BF16)
    drain()


def hand_over(nw, n1, n2, nw_out, n1_out, n2_out, sems):
    copies = [
        pltpu.make_async_copy(src, dst, sems.at[i])
        for i, (src, dst) in enumerate(((nw, nw_out), (n1, n1_out), (n2, n2_out)))
    ]
    for copy in copies:
        copy.start()
    for copy in copies:
        copy.wait()


def shards(tokens, cotangent, projection, weight, first_moment, second_moment):
    vmem = pl.BlockSpec(memory_space=pltpu.VMEM)
    hbm = pl.BlockSpec(memory_space=pltpu.HBM)
    dma = pltpu.SemaphoreType.DMA
    v = pltpu.VMEM
    scratch = [
        v(projection.shape, BF16),
        v(weight.shape, BF16),
        v(first_moment.shape, F32),
        v(second_moment.shape, F32),
        v((NX, RANK, WIDTH), BF16),
        v((NX, QUARTER, WIDTH), BF16),
        v((NX, QUARTER, WIDTH), BF16),
        tuple(v((NZ, RANK // NZ, n), BF16) for n in SIZES),
        tuple(v((NZ, RANK // NZ, n), BF16) for n in SIZES),
        tuple(v((2, RANK // NZ, n), BF16) for n in SIZES),
        tuple(v((NZ, RANK // NZ, n), BF16) for n in SIZES),
        v((NX, NY, 2, 32, WIDTH), F32),
        v((2, NX, NY, 16, WIDTH), BF16),
        v((2, NX, NY, 16, WIDTH), BF16),
        v((2, 2, NY, 16, WIDTH), BF16),
        v((2, 2, NY, 16, WIDTH), BF16),
        v((2, NY, 16, WIDTH), F32),
        v((2, NY, 16, WIDTH), BF16),
        v((2, NY, 16, WIDTH), BF16),
        v((NY, 2, 2, 16, WIDTH), BF16),
        v((NX, 16, RANK), BF16),
        v((NZ, NX, 16, RANK), BF16),
        v((2, 16, 16, RANK), BF16),
        v((2, NY, 16, WIDTH), F32),
        v((2, NY, 16, WIDTH), BF16),
        v((2, NY, 16, WIDTH), BF16),
        v((2, 16, WIDTH), BF16),
        v((2, 16, WIDTH), BF16),
        dma((6,)), dma(()),
        dma((1,)), dma((3,)), dma((1,)),
        dma((CHUNKS,)), dma((CHUNKS,)), dma((CHUNKS, 2)), dma((CHUNKS, 2)),
        dma((2, 3)), dma((2,)), dma((2,)), dma((2,)), dma((2,)), dma((2,)), dma((2,)),
        dma((1,)), dma((7,)), dma((1,)),
    ]
    shapes = (
        jax.ShapeDtypeStruct(weight.shape, weight.dtype),
        jax.ShapeDtypeStruct(first_moment.shape, F32),
        jax.ShapeDtypeStruct(second_moment.shape, F32),
    )
    results = pl.pallas_call(
        kernel,
        out_shape=tuple(v(t.shape, t.dtype) for t in shapes),
        in_specs=[hbm] * 6,
        out_specs=(vmem, vmem, vmem),
        scratch_shapes=scratch,
        compiler_params=pltpu.CompilerParams(
            collective_id=0, has_side_effects=True, vmem_limit_bytes=63 * 2**20
        ),
        cost_estimate=pl.CostEstimate(flops=1_800_000_000, bytes_accessed=4_500_000, transcendentals=8192),
    )(*(a.reshape(NX, QUARTER, WIDTH) for a in (tokens, cotangent)), projection, weight, first_moment, second_moment)
    return pl.pallas_call(
        hand_over,
        out_shape=shapes,
        in_specs=[vmem] * 3,
        out_specs=(hbm, hbm, hbm),
        scratch_shapes=[dma((3,))],
    )(*(pltpu.with_memory_space_constraint(r, pltpu.VMEM) for r in results))


def solution(mesh):
    return jax.shard_map(
        shards,
        mesh=mesh,
        in_specs=(
            P("dp", "fsdp"),
            P("dp", "fsdp"),
            P("fsdp", None),
            P("dp", "fsdp"),
            P("dp", "fsdp"),
            P("dp", "fsdp"),
        ),
        out_specs=(P("dp", "fsdp"), P("dp", "fsdp"), P("dp", "fsdp")),
        check_vma=False,
    )
```

```python
import functools

import jax
import jax.numpy as jnp
from jax import lax
from jax.experimental import pallas as pl
from jax.experimental.pallas import tpu as pltpu
from jax.sharding import PartitionSpec as P

STEP = 10
BETA_ONE = 0.9
BETA_TWO = 0.999
EPSILON = 1e-08
RATE = 0.1

NX, NY, NZ = 4, 8, 8
RANK = 512
WIDTH = 256
QUARTER = 768
SIZES = (128, 256, 256, 128)
CHUNKS = len(SIZES)
SUM_AT_ONCE = ()
GATHER_AT_ONCE = (CHUNKS - 1,)
STARTS = tuple(sum(SIZES[:k]) for k in range(CHUNKS))
MESH = pl.DeviceIdType.MESH
F32 = jnp.float32
BF16 = jnp.bfloat16


def kernel(
    tok, cot, proj_hbm, wgt_hbm, m1_hbm, m2_hbm, nw, n1, n2,
    proj, wgt, m1, m2, pt, t4, c4, psend, zr, zq, ag, acc, gs, gc, xs, xr, ysum, ys, yr, dirb,
    pu1, pu2, pu3, y2sum, y2s, y2r, x2s, x2r,
    lsem, s_out, s_pt, s_py, s_pc, s_t, s_c, s_z, s_a, s_g, s_x, s_y, s_y2, s_x2, s_d, s_dc, s_u1, s_u2, s_u3,
):
    dp = lax.axis_index("dp")
    fs = lax.axis_index("fsdp")
    y, c = dp // 2, lax.rem(dp, 2)
    x, z = fs // NZ, lax.rem(fs, NZ)
    o = 1 - c

    def px(d):
        return (dp, lax.rem(x + d + NX, NX) * NZ + z)

    def pz(d):
        return (dp, x * NZ + lax.rem(z + d + NZ, NZ))

    def py(d, other=False):
        return (lax.rem(y + d + NY, NY) * 2 + (o if other else c), fs)

    sent = []

    def put(src, dst, sem, dev):
        cp = pltpu.make_async_remote_copy(
            src_ref=src, dst_ref=dst, send_sem=s_out, recv_sem=sem, device_id=dev, device_id_type=MESH
        )
        cp.start()
        sent.append(cp)

    def drain(keep=0):
        while len(sent) > keep:
            sent.pop(0).wait_send()

    def got(dst, sem):
        pltpu.make_async_remote_copy(
            src_ref=dst, dst_ref=dst, send_sem=s_out, recv_sem=sem, device_id=(dp, fs), device_id_type=MESH
        ).wait_recv()

    barrier = pltpu.get_barrier_semaphore()
    for d in range(1, NX):
        pl.semaphore_signal(barrier, inc=1, device_id=px(d), device_id_type=MESH)
    for d in range(1, NZ):
        pl.semaphore_signal(barrier, inc=1, device_id=pz(d), device_id_type=MESH)
    for d in range(NY):
        pl.semaphore_signal(barrier, inc=1, device_id=py(d, True), device_id_type=MESH)
        if d:
            pl.semaphore_signal(barrier, inc=1, device_id=py(d), device_id_type=MESH)
    own_t = pltpu.make_async_copy(tok.at[x], t4.at[0], lsem.at[0])
    own_c = pltpu.make_async_copy(cot.at[x], c4.at[0], lsem.at[1])
    loads = [
        pltpu.make_async_copy(src, dst, lsem.at[i + 2])
        for i, (src, dst) in enumerate(((proj_hbm, proj), (wgt_hbm, wgt), (m1_hbm, m1), (m2_hbm, m2)))
    ]
    for load in loads:
        load.start()
    own_t.start()
    own_c.start()

    def send_tok(k):
        rows = pl.ds(STARTS[k], SIZES[k])
        for d in (2, 1, 3):
            put(tok.at[lax.rem(x + d, NX), rows], t4.at[d, rows], s_t.at[k], px(d))

    loads[0].wait()
    pt[0] = proj[...].T
    pu1[x] = proj[pl.ds(dp * 16, 16)]
    pl.semaphore_wait(barrier, NX - 1 + NZ - 1 + 2 * NY - 1)

    def ranks(core, row):
        return pl.ds(core * 256 + lax.rem(row + NY, 4) * 64, 64)

    others = pl.ds(1, NX - 1)
    for d in (2, 1, 3):
        put(pt.at[0, ranks(c, y)], pt.at[d, ranks(c, y)], s_pt.at[0], px(d))
    for d in (2, 1, 3):
        put(pu1.at[x], pu1.at[x], s_u1.at[0], px(d))
    for k in range(CHUNKS):
        send_tok(k)

    got(pt.at[others, ranks(c, y)], s_pt.at[0])
    far = 2 - 4 * c
    for i, d in enumerate((1, -1, far)):
        put(pt.at[others, ranks(c, y)], pt.at[others, ranks(c, y)], s_py.at[i], py(d))
    put(pt.at[others, ranks(c, y)], pt.at[others, ranks(c, y)], s_pc.at[0], py(0, True))

    got(pu1.at[others], s_u1.at[0])
    pu2[z] = pu1[...]

    def relay(step):
        up, down = lax.rem(z - step + 1 + NZ, NZ), lax.rem(z + step - 1, NZ)
        if step > 1:
            got(pu2.at[up], s_u2.at[step - 2])
            got(pu2.at[down], s_u2.at[step + 2])
        put(pu2.at[up], pu2.at[up], s_u2.at[step - 1], pz(1))
        if step < 4:
            put(pu2.at[down], pu2.at[down], s_u2.at[step + 3], pz(-1))

    relay(1)
    for i, d in enumerate((1, -1, far)):
        got(pt.at[others, ranks(c, y - d)], s_py.at[i])
        put(pt.at[others, ranks(c, y - d)], pt.at[others, ranks(c, y - d)], s_pc.at[0], py(0, True))
    relay(2)
    got(pt.at[others, pl.ds(o * 256, 256)], s_pc.at[0])
    own_t.wait()

    def send_cot():
        for k in range(CHUNKS):
            for d in (2, 1, 3):
                rows = pl.ds(STARTS[k], SIZES[k])
                put(cot.at[lax.rem(x + d, NX), rows], c4.at[d, rows], s_c.at[k], px(d))

    def at(d):
        return lax.rem(z + d + NZ, NZ)

    def sign(k):
        return 1 if k % 2 == 0 else -1

    def partial(k):
        rows = pl.ds(STARTS[k], SIZES[k])
        got(t4.at[others, rows], s_t.at[k])
        low = None
        for d in range(NX):
            part = lax.dot_general(
                pt[d], t4[d, rows], (((1,), (1,)), ((), ())), preferred_element_type=F32
            )
            low = part if low is None else low + part
        psend[k][...] = low.astype(BF16).reshape(NZ, RANK // NZ, SIZES[k])
        e = sign(k)
        if k in SUM_AT_ONCE:
            for d in (4, 3, 5, 2, 6, 1, 7):
                put(psend[k].at[at(d)], zr[k].at[d], s_z.at[k, 1], pz(d))
            return
        for owner, to, slot in ((-4, -e, 0), (-2 * e, e, 1), (e, -e, 2), (3 * e, e, 3), (-e, -e, 4)):
            put(psend[k].at[at(owner)], zr[k].at[slot], s_z.at[k, slot // 4], pz(to))

    def middle(k):
        e = sign(k)
        if k in SUM_AT_ONCE:
            return
        got(zr[k].at[pl.ds(0, 4)], s_z.at[k, 0])
        for owner, one, two, slot in ((-3 * e, 0, 1, 5), (2 * e, 2, 3, 6)):
            both = zr[k][one].astype(F32) + zr[k][two].astype(F32)
            zq[k][slot - 5] = (psend[k][at(owner)].astype(F32) + both).astype(BF16)
            put(zq[k].at[slot - 5], zr[k].at[slot], s_z.at[k, 1], pz(owner))

    def reduce(k):
        e = sign(k)
        total = psend[k][z].astype(F32)
        slots = range(1, NZ) if k in SUM_AT_ONCE else range(4, 7)
        got(zr[k].at[pl.ds(slots[0], len(slots))], s_z.at[k, 1])
        for slot in slots:
            total = total + zr[k][slot].astype(F32)
        ag[k][z] = total.astype(BF16)
        if k in GATHER_AT_ONCE:
            for d in (4, 3, 5, 2, 6, 1, 7):
                put(ag[k].at[z], ag[k].at[z], s_a.at[k, 1], pz(d))
            return
        for d in (3 * e, -2 * e, e):
            put(ag[k].at[z], ag[k].at[z], s_a.at[k, 1 if d == e else 0], pz(d))

    def forward(k):
        e = sign(k)
        if k in GATHER_AT_ONCE:
            return
        got(ag[k].at[pl.ds(0, 2)], s_a.at[k, 0])
        for d in (-2 * e, 3 * e):
            for f in (e, -e):
                put(ag[k].at[at(-d)], ag[k].at[at(-d)], s_a.at[k, 1], pz(f))

    def send_update_rows():
        got(pu2.at[lax.rem(z - 4 + NZ, NZ)], s_u2.at[3])
        for d in range(NY):
            for e in range(2):
                peer = lax.rem(y + d, NY) * 2 + (o if e else c)
                src = pu2.at[pl.ds(2 * lax.rem(peer, 4), 2), peer // 4]
                if d == 0 and e == 0:
                    pu3[:, dp] = pu2[pl.ds(2 * lax.rem(peer, 4), 2), peer // 4]
                else:
                    put(src, pu3.at[:, dp], s_u3.at[0], py(d, e == 1))

    for k in range(CHUNKS + 3):
        if k < CHUNKS:
            partial(k)
        if k == CHUNKS - 2:
            send_cot()
        if 0 <= k - 1 < CHUNKS:
            middle(k - 1)
        if 0 <= k - 2 < CHUNKS:
            reduce(k - 2)
        if 0 <= k - 3 < CHUNKS:
            forward(k - 3)
        if k < 2:
            relay(k + 3)
        if k == 2:
            send_update_rows()

    own_c.wait()
    for k in range(CHUNKS):
        rows = pl.ds(STARTS[k], SIZES[k])
        got(ag[k].at[pl.ds(0, 7 if k in GATHER_AT_ONCE else 5)], s_a.at[k, 1])
        if k == CHUNKS - 1:
            drain(3 * CHUNKS)
        got(c4.at[others, rows], s_c.at[k])
        low = ag[k][...].reshape(RANK, SIZES[k])
        for d in (2, 1, 3, 0):
            part = jnp.dot(low, c4[d, rows], preferred_element_type=F32).reshape(NY, 2, 32, WIDTH)
            acc[d] = part if k == 0 else acc[d] + part

    halves = (0, 1)
    order = (2, 1, 3, 0)
    groups = (pl.ds(0, 1), pl.ds(1, 2), pl.ds(3, 1))
    for h in halves:
        for i, group in enumerate(groups):
            for slot in range(group.start, group.start + group.size):
                gs[h, slot] = acc[order[slot], :, o, h * 16 : h * 16 + 16].astype(BF16)
            put(gs.at[h, group], gc.at[h, group], s_g.at[h, i], py(0, True))

    def paired(h, slot):
        return acc[order[slot], :, c, h * 16 : h * 16 + 16] + gc[h, slot].astype(F32)

    for h in halves:
        got(gc.at[h, groups[0]], s_g.at[h, 0])
        total = paired(h, 0)
        y2sum[h] = total
        y2s[h] = total.astype(BF16)
        for d in (4, 3, 5, 2, 6, 1, 7):
            put(y2s.at[h, lax.rem(y + d, NY)], y2r.at[h, d], s_y2.at[h], py(d))
        got(gc.at[h, groups[1]], s_g.at[h, 1])
        for slot in (1, 2):
            xs[h, slot - 1] = paired(h, slot).astype(BF16)
            put(xs.at[h, slot - 1], xr.at[h, slot - 1], s_x.at[h], px(-order[slot]))
    drain(22)
    for h in halves:
        got(gc.at[h, groups[2]], s_g.at[h, 2])
        total = paired(h, 3)
        got(xr.at[h], s_x.at[h])
        total = total + xr[h, 0].astype(F32) + xr[h, 1].astype(F32)
        ysum[h] = total
        ys[h] = total.astype(BF16)
        for d in (4, 3, 5, 2, 6, 1, 7):
            put(ys.at[h, lax.rem(y + d, NY)], yr.at[h, d], s_y.at[h], py(d))
    drain(14)
    for h in halves:
        got(y2r.at[h, pl.ds(1, NY - 1)], s_y2.at[h])
        total = y2sum[h, y]
        for d in range(1, NY):
            total = total + y2r[h, d].astype(F32)
        x2s[h] = total.astype(BF16)
        put(x2s.at[h], x2r.at[h], s_x2.at[h], px(2))
    for load in loads[1:]:
        load.wait()
    first_fix = 1.0 - BETA_ONE**STEP
    second_fix = 1.0 - BETA_TWO**STEP
    for h in halves:
        got(yr.at[h, pl.ds(1, NY - 1)], s_y.at[h])
        got(x2r.at[h], s_x2.at[h])
        gradient = ysum[h, y] + x2r[h].astype(F32)
        for d in range(1, NY):
            gradient = gradient + yr[h, d].astype(F32)
        rows = pl.ds(h * 16, 16)
        new_first = BETA_ONE * m1[rows] + (1.0 - BETA_ONE) * gradient
        new_second = BETA_TWO * m2[rows] + (1.0 - BETA_TWO) * gradient * gradient
        direction = new_first / first_fix / (jnp.sqrt(new_second / second_fix) + EPSILON)
        dirb[y, c, h] = direction.astype(BF16)
        for d in (4, 3, 5, 2, 6, 1, 7):
            put(dirb.at[y, c, h], dirb.at[y, c, h], s_d.at[h], py(d))
        n1[rows] = new_first
        n2[rows] = new_second
    drain(14)
    got(pu3.at[:, pl.ds(0, 2 * NY - 1)], s_u3.at[0])
    for h in halves:
        got(dirb.at[pl.ds(0, NY - 1), c, h], s_d.at[h])
        put(dirb.at[:, c, h], dirb.at[:, c, h], s_dc.at[h], py(0, True))
    for h in halves:
        got(dirb.at[:, o, h], s_dc.at[h])
    update = jnp.dot(
        pu3[...].reshape(RANK, RANK), dirb[...].reshape(RANK, WIDTH), preferred_element_type=F32
    )
    nw[...] = (wgt[...].astype(F32) - RATE * update).astype(BF16)
    drain()


def hand_over(nw, n1, n2, nw_out, n1_out, n2_out, sems):
    copies = [
        pltpu.make_async_copy(src, dst, sems.at[i])
        for i, (src, dst) in enumerate(((nw, nw_out), (n1, n1_out), (n2, n2_out)))
    ]
    for copy in copies:
        copy.start()
    for copy in copies:
        copy.wait()


def shards(tokens, cotangent, projection, weight, first_moment, second_moment):
    vmem = pl.BlockSpec(memory_space=pltpu.VMEM)
    hbm = pl.BlockSpec(memory_space=pltpu.HBM)
    dma = pltpu.SemaphoreType.DMA
    v = pltpu.VMEM
    scratch = [
        v(projection.shape, BF16),
        v(weight.shape, BF16),
        v(first_moment.shape, F32),
        v(second_moment.shape, F32),
        v((NX, RANK, WIDTH), BF16),
        v((NX, QUARTER, WIDTH), BF16),
        v((NX, QUARTER, WIDTH), BF16),
        tuple(v((NZ, RANK // NZ, n), BF16) for n in SIZES),
        tuple(v((NZ, RANK // NZ, n), BF16) for n in SIZES),
        tuple(v((2, RANK // NZ, n), BF16) for n in SIZES),
        tuple(v((NZ, RANK // NZ, n), BF16) for n in SIZES),
        v((NX, NY, 2, 32, WIDTH), F32),
        v((2, NX, NY, 16, WIDTH), BF16),
        v((2, NX, NY, 16, WIDTH), BF16),
        v((2, 2, NY, 16, WIDTH), BF16),
        v((2, 2, NY, 16, WIDTH), BF16),
        v((2, NY, 16, WIDTH), F32),
        v((2, NY, 16, WIDTH), BF16),
        v((2, NY, 16, WIDTH), BF16),
        v((NY, 2, 2, 16, WIDTH), BF16),
        v((NX, 16, RANK), BF16),
        v((NZ, NX, 16, RANK), BF16),
        v((2, 16, 16, RANK), BF16),
        v((2, NY, 16, WIDTH), F32),
        v((2, NY, 16, WIDTH), BF16),
        v((2, NY, 16, WIDTH), BF16),
        v((2, 16, WIDTH), BF16),
        v((2, 16, WIDTH), BF16),
        dma((6,)), dma(()),
        dma((1,)), dma((3,)), dma((1,)),
        dma((CHUNKS,)), dma((CHUNKS,)), dma((CHUNKS, 2)), dma((CHUNKS, 2)),
        dma((2, 3)), dma((2,)), dma((2,)), dma((2,)), dma((2,)), dma((2,)), dma((2,)),
        dma((1,)), dma((7,)), dma((1,)),
    ]
    shapes = (
        jax.ShapeDtypeStruct(weight.shape, weight.dtype),
        jax.ShapeDtypeStruct(first_moment.shape, F32),
        jax.ShapeDtypeStruct(second_moment.shape, F32),
    )
    results = pl.pallas_call(
        kernel,
        out_shape=tuple(v(t.shape, t.dtype) for t in shapes),
        in_specs=[hbm] * 6,
        out_specs=(vmem, vmem, vmem),
        scratch_shapes=scratch,
        compiler_params=pltpu.CompilerParams(
            collective_id=0, has_side_effects=True, vmem_limit_bytes=63 * 2**20
        ),
        cost_estimate=pl.CostEstimate(flops=1_800_000_000, bytes_accessed=4_500_000, transcendentals=8192),
    )(*(a.reshape(NX, QUARTER, WIDTH) for a in (tokens, cotangent)), projection, weight, first_moment, second_moment)
    return pl.pallas_call(
        hand_over,
        out_shape=shapes,
        in_specs=[vmem] * 3,
        out_specs=(hbm, hbm, hbm),
        scratch_shapes=[dma((3,))],
    )(*(pltpu.with_memory_space_constraint(r, pltpu.VMEM) for r in results))


def solution(mesh):
    return jax.shard_map(
        shards,
        mesh=mesh,
        in_specs=(
            P("dp", "fsdp"),
            P("dp", "fsdp"),
            P("fsdp", None),
            P("dp", "fsdp"),
            P("dp", "fsdp"),
            P("dp", "fsdp"),
        ),
        out_specs=(P("dp", "fsdp"), P("dp", "fsdp"), P("dp", "fsdp")),
        check_vma=False,
    )
```

```python
import functools

import jax
import jax.numpy as jnp
from jax import lax
from jax.experimental import pallas as pl
from jax.experimental.pallas import tpu as pltpu
from jax.sharding import PartitionSpec as P

STEP = 10
BETA_ONE = 0.9
BETA_TWO = 0.999
EPSILON = 1e-08
RATE = 0.1

NX, NY, NZ = 4, 8, 8
RANK = 512
WIDTH = 256
QUARTER = 768
SIZES = (128, 256, 256, 128)
CHUNKS = len(SIZES)
SUM_AT_ONCE = ()
GATHER_AT_ONCE = (CHUNKS - 1,)
STARTS = tuple(sum(SIZES[:k]) for k in range(CHUNKS))
MESH = pl.DeviceIdType.MESH
F32 = jnp.float32
BF16 = jnp.bfloat16


def kernel(
    tok, cot, proj_hbm, wgt_hbm, m1_hbm, m2_hbm, nw, n1, n2,
    proj, wgt, m1, m2, pt, t4, c4, psend, zr, zq, ag, acc, gs, gc, xs, xr, ysum, ys, yr, dirb,
    pu1, pu2, pu3, y2sum, y2s, y2r, x2s, x2r,
    lsem, s_out, s_pt, s_py, s_pc, s_t, s_c, s_z, s_a, s_g, s_x, s_y, s_y2, s_x2, s_d, s_dc, s_u1, s_u2, s_u3,
):
    dp = lax.axis_index("dp")
    fs = lax.axis_index("fsdp")
    y, c = dp // 2, lax.rem(dp, 2)
    x, z = fs // NZ, lax.rem(fs, NZ)
    o = 1 - c

    def px(d):
        return (dp, lax.rem(x + d + NX, NX) * NZ + z)

    def pz(d):
        return (dp, x * NZ + lax.rem(z + d + NZ, NZ))

    def py(d, other=False):
        return (lax.rem(y + d + NY, NY) * 2 + (o if other else c), fs)

    sent = []

    def put(src, dst, sem, dev):
        cp = pltpu.make_async_remote_copy(
            src_ref=src, dst_ref=dst, send_sem=s_out, recv_sem=sem, device_id=dev, device_id_type=MESH
        )
        cp.start()
        sent.append(cp)

    def drain(keep=0):
        while len(sent) > keep:
            sent.pop(0).wait_send()

    def got(dst, sem):
        pltpu.make_async_remote_copy(
            src_ref=dst, dst_ref=dst, send_sem=s_out, recv_sem=sem, device_id=(dp, fs), device_id_type=MESH
        ).wait_recv()

    barrier = pltpu.get_barrier_semaphore()
    for d in range(1, NX):
        pl.semaphore_signal(barrier, inc=1, device_id=px(d), device_id_type=MESH)
    for d in range(1, NZ):
        pl.semaphore_signal(barrier, inc=1, device_id=pz(d), device_id_type=MESH)
    for d in range(NY):
        pl.semaphore_signal(barrier, inc=1, device_id=py(d, True), device_id_type=MESH)
        if d:
            pl.semaphore_signal(barrier, inc=1, device_id=py(d), device_id_type=MESH)
    own_t = pltpu.make_async_copy(tok.at[x], t4.at[0], lsem.at[0])
    own_c = pltpu.make_async_copy(cot.at[x], c4.at[0], lsem.at[1])
    loads = [
        pltpu.make_async_copy(src, dst, lsem.at[i + 2])
        for i, (src, dst) in enumerate(((proj_hbm, proj), (wgt_hbm, wgt), (m1_hbm, m1), (m2_hbm, m2)))
    ]
    for load in loads:
        load.start()
    own_t.start()
    own_c.start()

    def send_tok(k):
        rows = pl.ds(STARTS[k], SIZES[k])
        for d in (2, 1, 3):
            put(tok.at[lax.rem(x + d, NX), rows], t4.at[d, rows], s_t.at[k], px(d))

    loads[0].wait()
    pt[0] = proj[...].T
    pu1[x] = proj[pl.ds(dp * 16, 16)]
    pl.semaphore_wait(barrier, NX - 1 + NZ - 1 + 2 * NY - 1)

    def ranks(core, row):
        return pl.ds(core * 256 + lax.rem(row + NY, 4) * 64, 64)

    others = pl.ds(1, NX - 1)
    for d in (2, 1, 3):
        put(pt.at[0, ranks(c, y)], pt.at[d, ranks(c, y)], s_pt.at[0], px(d))
    for d in (2, 1, 3):
        put(pu1.at[x], pu1.at[x], s_u1.at[0], px(d))
    for k in range(CHUNKS):
        send_tok(k)

    got(pt.at[others, ranks(c, y)], s_pt.at[0])
    far = 2 - 4 * c
    for i, d in enumerate((1, -1, far)):
        put(pt.at[others, ranks(c, y)], pt.at[others, ranks(c, y)], s_py.at[i], py(d))
    put(pt.at[others, ranks(c, y)], pt.at[others, ranks(c, y)], s_pc.at[0], py(0, True))

    got(pu1.at[others], s_u1.at[0])
    pu2[z] = pu1[...]

    def relay(step):
        up, down = lax.rem(z - step + 1 + NZ, NZ), lax.rem(z + step - 1, NZ)
        if step > 1:
            got(pu2.at[up], s_u2.at[step - 2])
            got(pu2.at[down], s_u2.at[step + 2])
        put(pu2.at[up], pu2.at[up], s_u2.at[step - 1], pz(1))
        if step < 4:
            put(pu2.at[down], pu2.at[down], s_u2.at[step + 3], pz(-1))

    relay(1)
    for i, d in enumerate((1, -1, far)):
        got(pt.at[others, ranks(c, y - d)], s_py.at[i])
        put(pt.at[others, ranks(c, y - d)], pt.at[others, ranks(c, y - d)], s_pc.at[0], py(0, True))
    relay(2)
    got(pt.at[others, pl.ds(o * 256, 256)], s_pc.at[0])
    own_t.wait()

    def send_cot():
        for k in range(CHUNKS):
            for d in (2, 1, 3):
                rows = pl.ds(STARTS[k], SIZES[k])
                put(cot.at[lax.rem(x + d, NX), rows], c4.at[d, rows], s_c.at[k], px(d))

    def at(d):
        return lax.rem(z + d + NZ, NZ)

    def sign(k):
        return 1 if k % 2 == 0 else -1

    def partial(k):
        rows = pl.ds(STARTS[k], SIZES[k])
        got(t4.at[others, rows], s_t.at[k])
        low = None
        for d in range(NX):
            part = lax.dot_general(
                pt[d], t4[d, rows], (((1,), (1,)), ((), ())), preferred_element_type=F32
            )
            low = part if low is None else low + part
        psend[k][...] = low.astype(BF16).reshape(NZ, RANK // NZ, SIZES[k])
        e = sign(k)
        if k in SUM_AT_ONCE:
            for d in (4, 3, 5, 2, 6, 1, 7):
                put(psend[k].at[at(d)], zr[k].at[d], s_z.at[k, 1], pz(d))
            return
        for owner, to, slot in ((-4, -e, 0), (-2 * e, e, 1), (e, -e, 2), (3 * e, e, 3), (-e, -e, 4)):
            put(psend[k].at[at(owner)], zr[k].at[slot], s_z.at[k, slot // 4], pz(to))

    def middle(k):
        e = sign(k)
        if k in SUM_AT_ONCE:
            return
        got(zr[k].at[pl.ds(0, 4)], s_z.at[k, 0])
        for owner, one, two, slot in ((-3 * e, 0, 1, 5), (2 * e, 2, 3, 6)):
            both = zr[k][one].astype(F32) + zr[k][two].astype(F32)
            zq[k][slot - 5] = (psend[k][at(owner)].astype(F32) + both).astype(BF16)
            put(zq[k].at[slot - 5], zr[k].at[slot], s_z.at[k, 1], pz(owner))

    def reduce(k):
        e = sign(k)
        total = psend[k][z].astype(F32)
        slots = range(1, NZ) if k in SUM_AT_ONCE else range(4, 7)
        got(zr[k].at[pl.ds(slots[0], len(slots))], s_z.at[k, 1])
        for slot in slots:
            total = total + zr[k][slot].astype(F32)
        ag[k][z] = total.astype(BF16)
        if k in GATHER_AT_ONCE:
            for d in (4, 3, 5, 2, 6, 1, 7):
                put(ag[k].at[z], ag[k].at[z], s_a.at[k, 1], pz(d))
            return
        for d in (3 * e, -2 * e, e):
            put(ag[k].at[z], ag[k].at[z], s_a.at[k, 1 if d == e else 0], pz(d))

    def forward(k):
        e = sign(k)
        if k in GATHER_AT_ONCE:
            return
        got(ag[k].at[pl.ds(0, 2)], s_a.at[k, 0])
        for d in (-2 * e, 3 * e):
            for f in (e, -e):
                put(ag[k].at[at(-d)], ag[k].at[at(-d)], s_a.at[k, 1], pz(f))

    def send_update_rows():
        got(pu2.at[lax.rem(z - 4 + NZ, NZ)], s_u2.at[3])
        for d in range(NY):
            for e in range(2):
                peer = lax.rem(y + d, NY) * 2 + (o if e else c)
                src = pu2.at[pl.ds(2 * lax.rem(peer, 4), 2), peer // 4]
                if d == 0 and e == 0:
                    pu3[:, dp] = pu2[pl.ds(2 * lax.rem(peer, 4), 2), peer // 4]
                else:
                    put(src, pu3.at[:, dp], s_u3.at[0], py(d, e == 1))

    for k in range(CHUNKS + 4):
        if k < CHUNKS:
            partial(k)
        if k == CHUNKS - 2:
            send_cot()
        if 0 <= k - 1 < CHUNKS:
            middle(k - 1)
        if 0 <= k - 2 < CHUNKS:
            reduce(k - 2)
        if 0 <= k - 4 < CHUNKS:
            forward(k - 4)
        if k < 2:
            relay(k + 3)
        if k == 2:
            send_update_rows()

    own_c.wait()
    for k in range(CHUNKS):
        rows = pl.ds(STARTS[k], SIZES[k])
        got(ag[k].at[pl.ds(0, 7 if k in GATHER_AT_ONCE else 5)], s_a.at[k, 1])
        if k == CHUNKS - 1:
            drain(3 * CHUNKS)
        got(c4.at[others, rows], s_c.at[k])
        low = ag[k][...].reshape(RANK, SIZES[k])
        for d in (2, 1, 3, 0):
            part = jnp.dot(low, c4[d, rows], preferred_element_type=F32).reshape(NY, 2, 32, WIDTH)
            acc[d] = part if k == 0 else acc[d] + part

    halves = (0, 1)
    order = (2, 1, 3, 0)
    groups = (pl.ds(0, 1), pl.ds(1, 2), pl.ds(3, 1))
    for h in halves:
        for i, group in enumerate(groups):
            for slot in range(group.start, group.start + group.size):
                gs[h, slot] = acc[order[slot], :, o, h * 16 : h * 16 + 16].astype(BF16)
            put(gs.at[h, group], gc.at[h, group], s_g.at[h, i], py(0, True))

    def paired(h, slot):
        return acc[order[slot], :, c, h * 16 : h * 16 + 16] + gc[h, slot].astype(F32)

    for h in halves:
        got(gc.at[h, groups[0]], s_g.at[h, 0])
        total = paired(h, 0)
        y2sum[h] = total
        y2s[h] = total.astype(BF16)
        for d in (4, 3, 5, 2, 6, 1, 7):
            put(y2s.at[h, lax.rem(y + d, NY)], y2r.at[h, d], s_y2.at[h], py(d))
        got(gc.at[h, groups[1]], s_g.at[h, 1])
        for slot in (1, 2):
            xs[h, slot - 1] = paired(h, slot).astype(BF16)
            put(xs.at[h, slot - 1], xr.at[h, slot - 1], s_x.at[h], px(-order[slot]))
    drain(22)
    for h in halves:
        got(gc.at[h, groups[2]], s_g.at[h, 2])
        total = paired(h, 3)
        got(xr.at[h], s_x.at[h])
        total = total + xr[h, 0].astype(F32) + xr[h, 1].astype(F32)
        ysum[h] = total
        ys[h] = total.astype(BF16)
        for d in (4, 3, 5, 2, 6, 1, 7):
            put(ys.at[h, lax.rem(y + d, NY)], yr.at[h, d], s_y.at[h], py(d))
    drain(14)
    for h in halves:
        got(y2r.at[h, pl.ds(1, NY - 1)], s_y2.at[h])
        total = y2sum[h, y]
        for d in range(1, NY):
            total = total + y2r[h, d].astype(F32)
        x2s[h] = total.astype(BF16)
        put(x2s.at[h], x2r.at[h], s_x2.at[h], px(2))
    for load in loads[1:]:
        load.wait()
    first_fix = 1.0 - BETA_ONE**STEP
    second_fix = 1.0 - BETA_TWO**STEP
    for h in halves:
        got(yr.at[h, pl.ds(1, NY - 1)], s_y.at[h])
        got(x2r.at[h], s_x2.at[h])
        gradient = ysum[h, y] + x2r[h].astype(F32)
        for d in range(1, NY):
            gradient = gradient + yr[h, d].astype(F32)
        rows = pl.ds(h * 16, 16)
        new_first = BETA_ONE * m1[rows] + (1.0 - BETA_ONE) * gradient
        new_second = BETA_TWO * m2[rows] + (1.0 - BETA_TWO) * gradient * gradient
        direction = new_first / first_fix / (jnp.sqrt(new_second / second_fix) + EPSILON)
        dirb[y, c, h] = direction.astype(BF16)
        for d in (4, 3, 5, 2, 6, 1, 7):
            put(dirb.at[y, c, h], dirb.at[y, c, h], s_d.at[h], py(d))
        n1[rows] = new_first
        n2[rows] = new_second
    drain(14)
    got(pu3.at[:, pl.ds(0, 2 * NY - 1)], s_u3.at[0])
    for h in halves:
        got(dirb.at[pl.ds(0, NY - 1), c, h], s_d.at[h])
        put(dirb.at[:, c, h], dirb.at[:, c, h], s_dc.at[h], py(0, True))
    for h in halves:
        got(dirb.at[:, o, h], s_dc.at[h])
    update = jnp.dot(
        pu3[...].reshape(RANK, RANK), dirb[...].reshape(RANK, WIDTH), preferred_element_type=F32
    )
    nw[...] = (wgt[...].astype(F32) - RATE * update).astype(BF16)
    drain()


def hand_over(nw, n1, n2, nw_out, n1_out, n2_out, sems):
    copies = [
        pltpu.make_async_copy(src, dst, sems.at[i])
        for i, (src, dst) in enumerate(((nw, nw_out), (n1, n1_out), (n2, n2_out)))
    ]
    for copy in copies:
        copy.start()
    for copy in copies:
        copy.wait()


def shards(tokens, cotangent, projection, weight, first_moment, second_moment):
    vmem = pl.BlockSpec(memory_space=pltpu.VMEM)
    hbm = pl.BlockSpec(memory_space=pltpu.HBM)
    dma = pltpu.SemaphoreType.DMA
    v = pltpu.VMEM
    scratch = [
        v(projection.shape, BF16),
        v(weight.shape, BF16),
        v(first_moment.shape, F32),
        v(second_moment.shape, F32),
        v((NX, RANK, WIDTH), BF16),
        v((NX, QUARTER, WIDTH), BF16),
        v((NX, QUARTER, WIDTH), BF16),
        tuple(v((NZ, RANK // NZ, n), BF16) for n in SIZES),
        tuple(v((NZ, RANK // NZ, n), BF16) for n in SIZES),
        tuple(v((2, RANK // NZ, n), BF16) for n in SIZES),
        tuple(v((NZ, RANK // NZ, n), BF16) for n in SIZES),
        v((NX, NY, 2, 32, WIDTH), F32),
        v((2, NX, NY, 16, WIDTH), BF16),
        v((2, NX, NY, 16, WIDTH), BF16),
        v((2, 2, NY, 16, WIDTH), BF16),
        v((2, 2, NY, 16, WIDTH), BF16),
        v((2, NY, 16, WIDTH), F32),
        v((2, NY, 16, WIDTH), BF16),
        v((2, NY, 16, WIDTH), BF16),
        v((NY, 2, 2, 16, WIDTH), BF16),
        v((NX, 16, RANK), BF16),
        v((NZ, NX, 16, RANK), BF16),
        v((2, 16, 16, RANK), BF16),
        v((2, NY, 16, WIDTH), F32),
        v((2, NY, 16, WIDTH), BF16),
        v((2, NY, 16, WIDTH), BF16),
        v((2, 16, WIDTH), BF16),
        v((2, 16, WIDTH), BF16),
        dma((6,)), dma(()),
        dma((1,)), dma((3,)), dma((1,)),
        dma((CHUNKS,)), dma((CHUNKS,)), dma((CHUNKS, 2)), dma((CHUNKS, 2)),
        dma((2, 3)), dma((2,)), dma((2,)), dma((2,)), dma((2,)), dma((2,)), dma((2,)),
        dma((1,)), dma((7,)), dma((1,)),
    ]
    shapes = (
        jax.ShapeDtypeStruct(weight.shape, weight.dtype),
        jax.ShapeDtypeStruct(first_moment.shape, F32),
        jax.ShapeDtypeStruct(second_moment.shape, F32),
    )
    results = pl.pallas_call(
        kernel,
        out_shape=tuple(v(t.shape, t.dtype) for t in shapes),
        in_specs=[hbm] * 6,
        out_specs=(vmem, vmem, vmem),
        scratch_shapes=scratch,
        compiler_params=pltpu.CompilerParams(
            collective_id=0, has_side_effects=True, vmem_limit_bytes=63 * 2**20
        ),
        cost_estimate=pl.CostEstimate(flops=1_800_000_000, bytes_accessed=4_500_000, transcendentals=8192),
    )(*(a.reshape(NX, QUARTER, WIDTH) for a in (tokens, cotangent)), projection, weight, first_moment, second_moment)
    return pl.pallas_call(
        hand_over,
        out_shape=shapes,
        in_specs=[vmem] * 3,
        out_specs=(hbm, hbm, hbm),
        scratch_shapes=[dma((3,))],
    )(*(pltpu.with_memory_space_constraint(r, pltpu.VMEM) for r in results))


def solution(mesh):
    return jax.shard_map(
        shards,
        mesh=mesh,
        in_specs=(
            P("dp", "fsdp"),
            P("dp", "fsdp"),
            P("fsdp", None),
            P("dp", "fsdp"),
            P("dp", "fsdp"),
            P("dp", "fsdp"),
        ),
        out_specs=(P("dp", "fsdp"), P("dp", "fsdp"), P("dp", "fsdp")),
        check_vma=False,
    )
```
